128 devices in a mesh: dp: 32 (over y, x, core), tensor: 4 (over z).
Axes of the slice: x: 4, y: 4, z: 4, core: 2. Of those that a mesh axis runs over, the one named last changes fastest.
Arguments:
- activations: bfloat16 [32768, 3584], P('dp'), may hold values from -60 to 60
- out_grads: bfloat16 [32768, 3584], P('dp', 'tensor'), may hold values from -6 to 6
- error_buffer: bfloat16 [32, 3584, 3584], P('dp', None, 'tensor'), may hold values from -6 to 6
- basis_q: float32 [3584, 32], P('tensor'), may hold values from -6 to 6
Outputs:
- update: bfloat16 [3584, 3584], P(None, 'tensor')
- new_error: bfloat16 [32, 3584, 3584], P('dp', None, 'tensor')
- next_q: float32 [3584, 32], P('tensor')
The draws below stay inside these ranges and needn't reach their ends.
All inputs are finite; a program needn't handle non-finite values.
Results may differ from the reference program's by a relative error of at most 0.001.
Values sent between devices are 32-bit elements; how exact they have to be, the bound alone decides.
A program may use at most 128 MiB of HBM per device.

```python
import jax
import jax.numpy as jnp
from jax import lax

ROWS = 3584
COLS = 3584
RANK = 32
TOK_DEV = 1024
REPLICAS = 32
TOKENS = 32768


def draw_activations(key, part):
    key = jax.random.fold_in(key, 11)
    base_key, col_key, row_key = jax.random.split(key, 3)
    col_scale = jnp.exp(jax.random.uniform(col_key, (1, ROWS), jnp.float32, jnp.log(0.3), jnp.log(3.0)))
    row_scale = jnp.exp(jax.random.uniform(row_key, (TOKENS, 1), jnp.float32, jnp.log(0.5), jnp.log(2.0)))
    base = jnp.clip(jax.random.normal(base_key, (TOKENS, ROWS), jnp.float32), -6.0, 6.0)
    values = base * col_scale * row_scale
    return values.astype(jnp.bfloat16)


def block_scale(key, shape, shards, smallest, high):
    def one(position, shards_of):
        heights = jax.random.uniform(jax.random.fold_in(jax.random.fold_in(key, 6), position), (shards_of,), jnp.float32, smallest / len(shards), high / len(shards))
        return jnp.repeat(jnp.exp(heights), shape[position] // shards_of).reshape((-1,) + (1,) * (len(shape) - position - 1))

    gain = one(*shards[0])
    for cut in shards[1:]:
        gain = gain * one(*cut)
    return gain


def bell_draw(stream_key, extent, spread, bound, cuts=(), held_as=jnp.bfloat16):
    result = jax.random.normal(stream_key, extent, jnp.float32) * spread
    if len(cuts) > 0:
        result = block_scale(stream_key, extent, cuts, -0.22, 0.18) * result
    return jnp.clip(result, min=-bound, max=bound).astype(held_as)


def setup_inputs(seed: int = 0) -> dict:
    streams_of = jax.random.split(jax.random.key(seed), 5)
    return {
        "activations": draw_activations(jax.random.fold_in(streams_of[4], 71), 0),
        "out_grads": bell_draw(streams_of[1], (TOKENS, COLS), 1.0, 6.0, ((0, 32), (1, 4))),
        "error_buffer": bell_draw(streams_of[2], (REPLICAS, ROWS, COLS), 1.0, 6.0, ((0, 32), (2, 4))),
        "basis_q": bell_draw(streams_of[3], (COLS, RANK), 1.0, 6.0, ((0, 4),), jnp.float32),
    }


def corrected_of(acts, grads, errs):
    grad = lax.dot_general(acts.astype(jnp.float32), grads.astype(jnp.float32), (((0,), (0,)), ((), ())), preferred_element_type=jnp.float32)
    return grad / jnp.sqrt(jnp.float32(TOK_DEV)) + errs.astype(jnp.float32)

def reference(activations, out_grads, error_buffer, basis_q):
    acts = activations.reshape(REPLICAS, TOK_DEV, ROWS)
    grads = out_grads.reshape(REPLICAS, TOK_DEV, COLS)

    def add_p(total, items):
        corrected = corrected_of(items[0], items[1], items[2])
        return (total + jnp.dot(corrected, basis_q, precision=lax.Precision.HIGHEST), None)
    p_sum, _ = lax.scan(add_p, jnp.zeros((ROWS, RANK), jnp.float32), (acts, grads, error_buffer))
    gram = jnp.dot(p_sum.T, p_sum, precision=lax.Precision.HIGHEST)
    factor = jnp.linalg.cholesky(gram)
    p_hat = lax.linalg.triangular_solve(factor, p_sum, left_side=False, lower=True, transpose_a=True)

    def per_replica(items):
        corrected = corrected_of(items[0], items[1], items[2])
        q_local = jnp.dot(corrected.T, p_hat, precision=lax.Precision.HIGHEST)
        fresh = corrected - jnp.dot(p_hat, q_local.T, precision=lax.Precision.HIGHEST)
        return (q_local, fresh.astype(jnp.bfloat16))
    q_all, new_error = lax.map(per_replica, (acts, grads, error_buffer))
    next_q = lax.optimization_barrier(jnp.sum(q_all, axis=0)) / jnp.float32(REPLICAS)
    update = jnp.dot(p_hat, next_q.T, precision=lax.Precision.HIGHEST).astype(jnp.bfloat16)
    return (update, new_error, next_q)
```

```python
import jax
import jax.numpy as jnp
from jax import lax
from jax.experimental import pallas as pl
from jax.experimental.pallas import tpu as pltpu
from jax.sharding import PartitionSpec as P

MESH = pl.DeviceIdType.MESH
F32 = jnp.float32
BF16 = jnp.bfloat16

ROWS = 3584
COLS = 896
TOK = 1024
RANK = 32
HALF = RANK // 2
CHUNK = 512
N_CHUNK = ROWS // CHUNK
CHIPS = 64
DPS = 32
LANES = 128
P_TILES = 56
Q_TILES = 28
SCALE = 1.0 / 32.0

NN = (((1,), (0,)), ((), ()))
NT = (((1,), (1,)), ((), ()))
TN = (((0,), (0,)), ((), ()))


def mm(a, b, dims=NN):
    return lax.dot_general(a, b, dims, preferred_element_type=F32)


def split2(x):
    hi = x.astype(BF16)
    lo = (x - hi.astype(F32)).astype(BF16)
    return hi, lo


def split3(x):
    hi = x.astype(BF16)
    rest = x - hi.astype(F32)
    mid = rest.astype(BF16)
    lo = (rest - mid.astype(F32)).astype(BF16)
    return hi, mid, lo


def fold3(x):
    return x[:RANK] + x[RANK:2 * RANK] + x[2 * RANK:]


def inverse_factor(gram):
    row_id = lax.broadcasted_iota(jnp.int32, (RANK, LANES), 0)
    lane_id = lax.broadcasted_iota(jnp.int32, (RANK, LANES), 1)
    eye = (lane_id == row_id + RANK).astype(F32)
    work = jnp.concatenate([gram, jnp.zeros((RANK, LANES - RANK), F32)], axis=1) + eye
    scale = jnp.zeros((RANK, LANES), F32)
    for j in range(RANK):
        row = work[j:j + 1, :]
        piv = jnp.broadcast_to(work[j:j + 1, j:j + 1], (1, LANES))
        col = jnp.broadcast_to(work[:, j:j + 1], (RANK, LANES))
        scale = jnp.where(row_id == j, piv, scale)
        work = work - jnp.where(row_id > j, col * (row / piv), 0.0)
    return (work * lax.rsqrt(scale))[:, RANK:2 * RANK]


def body(a_hbm, g_hbm, e_hbm, q_ref, c_ref, phat_ref, qloc_ref, nextq_ref,
         a_buf, g_buf, e_buf, qs, gqs, p_loc, core_buf, p_sum, p_full, p_recv, psplit,
         q_raw, q_recv, q_full,
         a_sem, g_sem, e_sem, cs_sem, cr_sem, rs_send, rs_recv, ag_send, ag_recv,
         x_send, x_recv, qs_send, qs_recv, qa_send, qa_recv):
    dp = lax.axis_index("dp")
    z = lax.axis_index("tensor")
    core = dp % 2
    plane = dp // 2
    chip = plane * 4 + z
    sib = (plane * 2 + 1 - core, z)

    def chip_dev(k):
        return ((k // 4) * 2 + core, k % 4)

    g_copy = pltpu.make_async_copy(g_hbm, g_buf, g_sem)
    g_copy.start()
    a_copies = []
    e_copies = []
    for j in range(N_CHUNK):
        cols = pl.ds(j * CHUNK, CHUNK)
        a_copies.append(pltpu.make_async_copy(a_hbm.at[:, cols], a_buf.at[j], a_sem.at[j]))
        e_copies.append(pltpu.make_async_copy(e_hbm.at[cols, :], e_buf.at[cols, :], e_sem.at[j]))
        a_copies[j].start()
        e_copies[j].start()

    bar = pltpu.get_barrier_semaphore()
    pl.semaphore_signal(bar, inc=1, device_id=sib, device_id_type=MESH)

    @pl.loop(0, CHIPS)
    def _(k):
        @pl.when(k != chip)
        def _():
            pl.semaphore_signal(bar, inc=1, device_id=chip_dev(k), device_id_type=MESH)

    @pl.loop(0, DPS)
    def _(k):
        @pl.when(k % 2 != core)
        def _():
            @pl.when(k // 2 != plane)
            def _():
                pl.semaphore_signal(bar, inc=1, device_id=(k, z), device_id_type=MESH)

    for i, part in enumerate(split3(q_ref[...])):
        qs[i * RANK:(i + 1) * RANK, :] = part
    g_copy.wait()
    gq = fold3(mm(qs[...], g_buf[...], NT)) * SCALE
    for i, part in enumerate(split3(gq)):
        gqs[i * RANK:(i + 1) * RANK, :] = part

    mine = pl.multiple_of(core * HALF, HALF)
    other = pl.multiple_of(HALF - core * HALF, HALF)

    def core_copy(j):
        cols = pl.ds(j * CHUNK, CHUNK)
        return pltpu.make_async_remote_copy(
            src_ref=p_loc.at[pl.ds(other, HALF), cols], dst_ref=core_buf.at[:, cols],
            send_sem=cs_sem.at[j], recv_sem=cr_sem.at[j], device_id=sib, device_id_type=MESH)

    def scatter(j):
        cols = pl.ds(j * CHUNK, CHUNK)
        core_copy(j).wait_recv()
        p_sum[:, cols] = p_loc[pl.ds(mine, HALF), cols] + core_buf[:, cols]

        def send(i, carry):
            owner = i * 8 + j
            rows = pl.ds(pl.multiple_of((i // 4) * 8, 8), 8)
            lanes = pl.ds(pl.multiple_of(j * CHUNK + (i % 4) * LANES, LANES), LANES)

            @pl.when(owner != chip)
            def _():
                pltpu.make_async_remote_copy(
                    src_ref=p_sum.at[rows, lanes], dst_ref=p_recv.at[chip],
                    send_sem=rs_send, recv_sem=rs_recv,
                    device_id=chip_dev(owner), device_id_type=MESH).start()

            @pl.when(owner == chip)
            def _():
                p_recv[chip] = p_sum[rows, lanes]
            return carry
        lax.fori_loop(0, 8, send, 0)

    for j in range(N_CHUNK):
        cols = pl.ds(j * CHUNK, CHUNK)
        a_copies[j].wait()
        e_copies[j].wait()
        p_loc[:, cols] = fold3(mm(gqs[...], a_buf[j]) + mm(qs[...], e_buf[cols, :], NT))
        if j == 0:
            pl.semaphore_wait(bar, 1 + (CHIPS - 1) + (DPS // 2 - 1))
        core_copy(j).start()
        if j > 0:
            scatter(j - 1)

    def correct(j):
        cols = pl.ds(j * CHUNK, CHUNK)
        c_ref[cols, :] = mm(a_buf[j], g_buf[...], TN) * SCALE + e_buf[cols, :].astype(F32)

    correct(0)
    scatter(N_CHUNK - 1)
    for j in range(1, N_CHUNK):
        correct(j)

    t_i = chip // 8
    t_j = chip % 8
    owns = t_j < N_CHUNK
    t_rows = pl.ds(pl.multiple_of(core * HALF + (t_i // 4) * 8, 8), 8)
    t_lanes = pl.ds(pl.multiple_of(jnp.minimum(t_j, N_CHUNK - 1) * CHUNK + (t_i % 4) * LANES, LANES), LANES)

    @pl.when(owns)
    def _():
        got = p_recv.at[pl.ds(0, CHIPS - 1)]
        pltpu.make_async_copy(got, got, rs_recv).wait()
        p_full[t_rows, t_lanes] = jnp.sum(p_recv[...], axis=0)

        def send(k, carry):
            @pl.when(k != chip)
            def _():
                pltpu.make_async_remote_copy(
                    src_ref=p_full.at[t_rows, t_lanes], dst_ref=p_full.at[t_rows, t_lanes],
                    send_sem=ag_send, recv_sem=ag_recv,
                    device_id=chip_dev(k), device_id_type=MESH).start()
            return carry
        lax.fori_loop(0, CHIPS, send, 0)
        most = p_recv.at[pl.ds(0, P_TILES - 1)]
        pltpu.make_async_copy(most, most, ag_recv).wait()

    @pl.when(jnp.logical_not(owns))
    def _():
        most = p_recv.at[pl.ds(0, P_TILES)]
        pltpu.make_async_copy(most, most, ag_recv).wait()

    half = p_full.at[pl.ds(mine, HALF), :]
    swap = pltpu.make_async_remote_copy(
        src_ref=half, dst_ref=half, send_sem=x_send, recv_sem=x_recv,
        device_id=sib, device_id_type=MESH)
    swap.start()
    swap.wait()

    for i, part in enumerate(split3(p_full[...])):
        psplit[i * RANK:(i + 1) * RANK, :] = part
    acc = jnp.zeros((RANK, COLS), F32)
    for j in range(N_CHUNK):
        cols = pl.ds(j * CHUNK, CHUNK)
        hi, lo = split2(c_ref[cols, :])
        acc = acc + fold3(mm(psplit[:, cols], hi) + mm(psplit[:, cols], lo))
    q_raw[...] = acc

    def q_send(t, carry):
        rows = pl.ds(pl.multiple_of((t // 7) * 8, 8), 8)
        lanes = pl.ds(pl.multiple_of((t % 7) * LANES, LANES), LANES)

        @pl.when(t != dp)
        def _():
            pltpu.make_async_remote_copy(
                src_ref=q_raw.at[rows, lanes], dst_ref=q_recv.at[dp],
                send_sem=qs_send, recv_sem=qs_recv, device_id=(t, z), device_id_type=MESH).start()

        @pl.when(t == dp)
        def _():
            q_recv[dp] = q_raw[rows, lanes]
        return carry
    lax.fori_loop(0, Q_TILES, q_send, 0)

    gram9 = mm(psplit[...], psplit[...], NT)
    gram = jnp.zeros((RANK, RANK), F32)
    for r in range(3):
        for c in range(3):
            gram = gram + gram9[r * RANK:(r + 1) * RANK, c * RANK:(c + 1) * RANK]
    inv = inverse_factor(gram)

    q_owns = dp < Q_TILES
    t = jnp.minimum(dp, Q_TILES - 1)
    q_rows = pl.ds(pl.multiple_of((t // 7) * 8, 8), 8)
    q_lanes = pl.ds(pl.multiple_of((t % 7) * LANES, LANES), LANES)

    @pl.when(q_owns)
    def _():
        got = q_recv.at[pl.ds(0, DPS - 1)]
        pltpu.make_async_copy(got, got, qs_recv).wait()
        q_full[q_rows, q_lanes] = jnp.sum(q_recv[...], axis=0)

        def send(k, carry):
            @pl.when(k != dp)
            def _():
                pltpu.make_async_remote_copy(
                    src_ref=q_full.at[q_rows, q_lanes], dst_ref=q_full.at[q_rows, q_lanes],
                    send_sem=qa_send, recv_sem=qa_recv, device_id=(k, z), device_id_type=MESH).start()
            return carry
        lax.fori_loop(0, DPS, send, 0)

    inv_parts = split3(inv)
    inv_left = jnp.concatenate([inv_parts[0], inv_parts[0], inv_parts[1], inv_parts[0], inv_parts[1], inv_parts[2]], axis=1)

    def six(parts):
        return jnp.concatenate([parts[0], parts[1], parts[0], parts[2], parts[1], parts[0]], axis=0)

    p_hat = mm(inv_left, six((psplit[:RANK, :], psplit[RANK:2 * RANK, :], psplit[2 * RANK:, :])))
    ph = jnp.transpose(p_hat)
    ph_hi, ph_lo = split2(ph)
    phat_ref[:, :RANK] = ph_hi
    phat_ref[:, RANK:2 * RANK] = ph_hi
    phat_ref[:, 2 * RANK:] = ph_lo
    q_hi, q_lo = split2(mm(inv_left, six(split3(q_raw[...]))))
    qloc_ref[:RANK, :] = q_hi
    qloc_ref[RANK:2 * RANK, :] = q_lo
    qloc_ref[2 * RANK:, :] = q_hi

    @pl.when(q_owns)
    def _():
        most = q_recv.at[pl.ds(0, Q_TILES - 1)]
        pltpu.make_async_copy(most, most, qa_recv).wait()

    @pl.when(jnp.logical_not(q_owns))
    def _():
        most = q_recv.at[pl.ds(0, Q_TILES)]
        pltpu.make_async_copy(most, most, qa_recv).wait()

    nextq_ref[...] = mm(inv_left, six(split3(q_full[...]))) * (1.0 / DPS)

    for j in range(N_CHUNK):
        core_copy(j).wait_send()

    @pl.when(owns)
    def _():
        sent = p_recv.at[pl.ds(0, P_TILES - 1)]
        pltpu.make_async_copy(sent, sent, rs_send).wait()
        sent = p_recv.at[pl.ds(0, CHIPS - 1)]
        pltpu.make_async_copy(sent, sent, ag_send).wait()

    @pl.when(jnp.logical_not(owns))
    def _():
        sent = p_recv.at[pl.ds(0, P_TILES)]
        pltpu.make_async_copy(sent, sent, rs_send).wait()

    @pl.when(q_owns)
    def _():
        sent = q_recv.at[pl.ds(0, Q_TILES - 1)]
        pltpu.make_async_copy(sent, sent, qs_send).wait()
        sent = q_recv.at[pl.ds(0, DPS - 1)]
        pltpu.make_async_copy(sent, sent, qa_send).wait()

    @pl.when(jnp.logical_not(q_owns))
    def _():
        sent = q_recv.at[pl.ds(0, Q_TILES)]
        pltpu.make_async_copy(sent, sent, qs_send).wait()


def factors(a, g, e, q):
    vm = pl.BlockSpec(memory_space=pltpu.VMEM)
    hbm = pl.BlockSpec(memory_space=pltpu.HBM)
    dma = pltpu.SemaphoreType.DMA
    return pl.pallas_call(
        body,
        out_shape=(
            pltpu.VMEM((ROWS, COLS), F32),
            pltpu.VMEM((ROWS, 3 * RANK), BF16),
            pltpu.VMEM((3 * RANK, COLS), BF16),
            pltpu.VMEM((RANK, COLS), F32),
        ),
        in_specs=[hbm, hbm, hbm, vm],
        out_specs=(vm, vm, vm, vm),
        scratch_shapes=[
            pltpu.VMEM((N_CHUNK, TOK, CHUNK), BF16),
            pltpu.VMEM((TOK, COLS), BF16),
            pltpu.VMEM((ROWS, COLS), BF16),
            pltpu.VMEM((3 * RANK, COLS), BF16),
            pltpu.VMEM((3 * RANK, TOK), BF16),
            pltpu.VMEM((RANK, ROWS), F32),
            pltpu.VMEM((HALF, ROWS), F32),
            pltpu.VMEM((HALF, ROWS), F32),
            pltpu.VMEM((RANK, ROWS), F32),
            pltpu.VMEM((CHIPS, 8, LANES), F32),
            pltpu.VMEM((3 * RANK, ROWS), BF16),
            pltpu.VMEM((RANK, COLS), F32),
            pltpu.VMEM((DPS, 8, LANES), F32),
            pltpu.VMEM((RANK, COLS), F32),
            dma((N_CHUNK,)), dma, dma((N_CHUNK,)), dma((N_CHUNK,)), dma((N_CHUNK,)),
            dma, dma, dma, dma, dma, dma, dma, dma, dma, dma,
        ],
        compiler_params=pltpu.CompilerParams(
            collective_id=0, has_side_effects=True, vmem_limit_bytes=36 * 2**20),
        name="factors",
    )(a, g, e, q)


def out_body(c_ref, phat_ref, qloc_ref, nextq_ref, upd_ref, err_ref, nq_ref, nqs):
    @pl.when(pl.program_id(0) == 0)
    def _():
        hi, lo = split2(nextq_ref[...])
        nqs[:RANK, :] = hi
        nqs[RANK:2 * RANK, :] = lo
        nqs[2 * RANK:, :] = hi
        nq_ref[...] = nextq_ref[...]
    rows = pl.ds(pl.multiple_of(pl.program_id(0) * CHUNK, CHUNK), CHUNK)
    ph = phat_ref[rows, :]
    err_ref[...] = (c_ref[rows, :] - mm(ph, qloc_ref[...])).astype(BF16)
    upd_ref[...] = mm(ph, nqs[...]).astype(BF16)


def outputs(c, phat, qloc, nextq):
    vm = pl.BlockSpec(memory_space=pltpu.VMEM)
    block = pl.BlockSpec((CHUNK, COLS), lambda i: (i, 0))
    return pl.pallas_call(
        out_body,
        grid=(N_CHUNK,),
        out_shape=(
            jax.ShapeDtypeStruct((ROWS, COLS), BF16),
            jax.ShapeDtypeStruct((ROWS, COLS), BF16),
            jax.ShapeDtypeStruct((RANK, COLS), F32),
        ),
        in_specs=[vm, vm, vm, vm],
        out_specs=(block, block, pl.BlockSpec((RANK, COLS), lambda i: (0, 0))),
        scratch_shapes=[pltpu.VMEM((3 * RANK, COLS), BF16)],
        compiler_params=pltpu.CompilerParams(vmem_limit_bytes=24 * 2**20),
        name="outputs",
    )(c, phat, qloc, nextq)


def shards(activations, out_grads, error_buffer, basis_q):
    c, phat, qloc, nextq = factors(activations, out_grads, error_buffer[0], basis_q.T)
    update, new_error, next_q = outputs(c, phat, qloc, nextq)
    return update, new_error[None], next_q.T


def solution(mesh):
    in_specs = (P("dp", None), P("dp", "tensor"), P("dp", None, "tensor"), P("tensor", None))
    out_specs = (P(None, "tensor"), P("dp", None, "tensor"), P("tensor", None))
    return jax.shard_map(shards, mesh=mesh, in_specs=in_specs, out_specs=out_specs, check_vma=False)
```

```python
import jax
import jax.numpy as jnp
from jax import lax
from jax.experimental import pallas as pl
from jax.experimental.pallas import tpu as pltpu
from jax.sharding import PartitionSpec as P

MESH = pl.DeviceIdType.MESH
F32 = jnp.float32
BF16 = jnp.bfloat16

ROWS = 3584
COLS = 896
TOK = 1024
RANK = 32
HALF = RANK // 2
CHUNK = 512
N_CHUNK = ROWS // CHUNK
CHIPS = 64
DPS = 32
LANES = 128
P_TILES = 56
Q_TILES = 28
SCALE = 1.0 / 32.0
BAR_AT = 3
EARLY = 5

NN = (((1,), (0,)), ((), ()))
NT = (((1,), (1,)), ((), ()))
TN = (((0,), (0,)), ((), ()))


def mm(a, b, dims=NN):
    return lax.dot_general(a, b, dims, preferred_element_type=F32)


def split2(x):
    hi = x.astype(BF16)
    lo = (x - hi.astype(F32)).astype(BF16)
    return hi, lo


def split3(x):
    hi = x.astype(BF16)
    rest = x - hi.astype(F32)
    mid = rest.astype(BF16)
    lo = (rest - mid.astype(F32)).astype(BF16)
    return hi, mid, lo


def fold3(x):
    return x[:RANK] + x[RANK:2 * RANK] + x[2 * RANK:]


def inverse_factor(gram):
    row_id = lax.broadcasted_iota(jnp.int32, (RANK, LANES), 0)
    lane_id = lax.broadcasted_iota(jnp.int32, (RANK, LANES), 1)
    eye = (lane_id == row_id + RANK).astype(F32)
    work = jnp.concatenate([gram, jnp.zeros((RANK, LANES - RANK), F32)], axis=1) + eye
    scale = jnp.zeros((RANK, LANES), F32)
    for j in range(RANK):
        row = work[j:j + 1, :]
        piv = jnp.broadcast_to(work[j:j + 1, j:j + 1], (1, LANES))
        col = jnp.broadcast_to(work[:, j:j + 1], (RANK, LANES))
        scale = jnp.where(row_id == j, piv, scale)
        work = work - jnp.where(row_id > j, col * (row / piv), 0.0)
    return (work * lax.rsqrt(scale))[:, RANK:2 * RANK]


def far(i):
    return jnp.where(i < 2, 2 + i, 3 - i)


def body(a_hbm, g_hbm, e_hbm, q_hbm, err_ref, phat_ref, nextq_ref,
         a_buf, g_buf, e_buf, q_buf, c_hi, c_lo, qs, gqs, p_loc, core_buf, p_sum, p_full, p_recv, psplit,
         q_raw, q_recv, q_full,
         a_sem, g_sem, e_sem, q_sem, cs_sem, cr_sem, rs_send, rs_recv, ag_send, ag_recv,
         x_send, x_recv, qs_send, qs_recv, qa_send, qa_recv):
    dp = lax.axis_index("dp")
    z = lax.axis_index("tensor")
    core = dp % 2
    plane = dp // 2
    y = plane // 4
    x = plane % 4
    chip = plane * 4 + z
    sib = (plane * 2 + 1 - core, z)

    def chip_at(d):
        py = (y + far(d // 16)) % 4
        px = (x + far((d // 4) % 4)) % 4
        pz = (z + far(d % 4)) % 4
        return ((py * 4 + px) * 2 + core, pz)

    def dp_at(d):
        py = (y + far(d // 8)) % 4
        px = (x + far((d // 2) % 4)) % 4
        pc = (core + 1 - d % 2) % 2
        return (py * 4 + px) * 2 + pc

    q_copy = pltpu.make_async_copy(q_hbm, q_buf, q_sem)
    g_copy = pltpu.make_async_copy(g_hbm, g_buf, g_sem)
    q_copy.start()
    g_copy.start()
    a_copies = []
    e_copies = []
    for j in range(N_CHUNK):
        cols = pl.ds(j * CHUNK, CHUNK)
        a_copies.append(pltpu.make_async_copy(a_hbm.at[:, cols], a_buf.at[j], a_sem.at[j]))
        e_copies.append(pltpu.make_async_copy(e_hbm.at[cols, :], e_buf.at[cols, :], e_sem.at[j]))
        a_copies[j].start()
        e_copies[j].start()

    bar = pltpu.get_barrier_semaphore()
    pl.semaphore_signal(bar, inc=1, device_id=sib, device_id_type=MESH)

    @pl.loop(0, CHIPS - 1)
    def _(d):
        pl.semaphore_signal(bar, inc=1, device_id=chip_at(d), device_id_type=MESH)

    @pl.loop(0, DPS // 2 - 1)
    def _(d):
        pl.semaphore_signal(bar, inc=1, device_id=(dp_at(2 * d), z), device_id_type=MESH)

    q_copy.wait()
    for i, part in enumerate(split3(q_buf[...])):
        qs[i * RANK:(i + 1) * RANK, :] = part
    g_copy.wait()
    gq = fold3(mm(qs[...], g_buf[...], NT)) * SCALE
    for i, part in enumerate(split3(gq)):
        gqs[i * RANK:(i + 1) * RANK, :] = part

    mine = pl.multiple_of(core * HALF, HALF)
    other = pl.multiple_of(HALF - core * HALF, HALF)

    def core_copy(j):
        cols = pl.ds(j * CHUNK, CHUNK)
        return pltpu.make_async_remote_copy(
            src_ref=p_loc.at[pl.ds(other, HALF), cols], dst_ref=core_buf.at[:, cols],
            send_sem=cs_sem.at[j], recv_sem=cr_sem.at[j], device_id=sib, device_id_type=MESH)

    def scatter(j):
        cols = pl.ds(j * CHUNK, CHUNK)
        core_copy(j).wait_recv()
        p_sum[:, cols] = p_loc[pl.ds(mine, HALF), cols] + core_buf[:, cols]

        def send(n, carry):
            i = (n + chip // 8) % 8
            owner = i * 8 + j
            rows = pl.ds(pl.multiple_of((i // 4) * 8, 8), 8)
            lanes = pl.ds(pl.multiple_of(j * CHUNK + (i % 4) * LANES, LANES), LANES)

            @pl.when(owner != chip)
            def _():
                pltpu.make_async_remote_copy(
                    src_ref=p_sum.at[rows, lanes], dst_ref=p_recv.at[chip],
                    send_sem=rs_send, recv_sem=rs_recv,
                    device_id=((owner // 4) * 2 + core, owner % 4), device_id_type=MESH).start()

            @pl.when(owner == chip)
            def _():
                p_recv[chip] = p_sum[rows, lanes]
            return carry
        lax.fori_loop(0, 8, send, 0)

    for j in range(N_CHUNK):
        cols = pl.ds(j * CHUNK, CHUNK)
        a_copies[j].wait()
        e_copies[j].wait()
        p_loc[:, cols] = fold3(mm(gqs[...], a_buf[j]) + mm(qs[...], e_buf[cols, :], NT))
        if j == BAR_AT:
            pl.semaphore_wait(bar, 1 + (CHIPS - 1) + (DPS // 2 - 1))
            for i in range(BAR_AT):
                core_copy(i).start()
        if j >= BAR_AT:
            core_copy(j).start()
        if j > BAR_AT:
            for i in range(0 if j == BAR_AT + 1 else j - 1, j):
                scatter(i)

    def correct(j):
        cols = pl.ds(j * CHUNK, CHUNK)
        c = mm(a_buf[j], g_buf[...], TN) * SCALE + e_buf[cols, :].astype(F32)
        hi, lo = split2(c)
        c_hi[cols, :] = hi
        c_lo[cols, :] = lo

    correct(0)
    scatter(N_CHUNK - 1)
    for j in range(1, EARLY):
        correct(j)

    t_i = chip // 8
    t_j = chip % 8
    owns = t_j < N_CHUNK
    t_rows = pl.ds(pl.multiple_of(core * HALF + (t_i // 4) * 8, 8), 8)
    t_lanes = pl.ds(pl.multiple_of(jnp.minimum(t_j, N_CHUNK - 1) * CHUNK + (t_i % 4) * LANES, LANES), LANES)

    @pl.when(owns)
    def _():
        got = p_recv.at[pl.ds(0, CHIPS - 1)]
        pltpu.make_async_copy(got, got, rs_recv).wait()
        p_full[t_rows, t_lanes] = jnp.sum(p_recv[...], axis=0)

        def send(d, carry):
            pltpu.make_async_remote_copy(
                src_ref=p_full.at[t_rows, t_lanes], dst_ref=p_full.at[t_rows, t_lanes],
                send_sem=ag_send, recv_sem=ag_recv,
                device_id=chip_at(d), device_id_type=MESH).start()
            return carry
        lax.fori_loop(0, CHIPS - 1, send, 0)

    for j in range(EARLY, N_CHUNK):
        correct(j)

    @pl.when(owns)
    def _():
        most = p_recv.at[pl.ds(0, P_TILES - 1)]
        pltpu.make_async_copy(most, most, ag_recv).wait()

    @pl.when(jnp.logical_not(owns))
    def _():
        most = p_recv.at[pl.ds(0, P_TILES)]
        pltpu.make_async_copy(most, most, ag_recv).wait()

    half = p_full.at[pl.ds(mine, HALF), :]
    swap = pltpu.make_async_remote_copy(
        src_ref=half, dst_ref=half, send_sem=x_send, recv_sem=x_recv,
        device_id=sib, device_id_type=MESH)
    swap.start()
    swap.wait()

    for i, part in enumerate(split3(p_full[...])):
        psplit[i * RANK:(i + 1) * RANK, :] = part
    acc = jnp.zeros((3 * RANK, COLS), F32)
    for j in range(N_CHUNK):
        cols = pl.ds(j * CHUNK, CHUNK)
        acc = acc + (mm(psplit[:, cols], c_hi[cols, :]) + mm(psplit[:, cols], c_lo[cols, :]))
    q_raw[...] = fold3(acc)

    def q_send(d, carry):
        t = dp_at(d)
        rows = pl.ds(pl.multiple_of((t // 7) * 8, 8), 8)
        lanes = pl.ds(pl.multiple_of((t % 7) * LANES, LANES), LANES)

        @pl.when(t < Q_TILES)
        def _():
            pltpu.make_async_remote_copy(
                src_ref=q_raw.at[rows, lanes], dst_ref=q_recv.at[dp],
                send_sem=qs_send, recv_sem=qs_recv, device_id=(t, z), device_id_type=MESH).start()
        return carry
    lax.fori_loop(0, DPS - 1, q_send, 0)

    gram9 = mm(psplit[...], psplit[...], NT)
    gram = jnp.zeros((RANK, RANK), F32)
    for r in range(3):
        for c in range(3):
            gram = gram + gram9[r * RANK:(r + 1) * RANK, c * RANK:(c + 1) * RANK]
    inv = inverse_factor(gram)
    inv_parts = split3(inv)
    inv_left = jnp.concatenate([inv_parts[0], inv_parts[0], inv_parts[1], inv_parts[0], inv_parts[1], inv_parts[2]], axis=1)

    def six(parts):
        return jnp.concatenate([parts[0], parts[1], parts[0], parts[2], parts[1], parts[0]], axis=0)

    q_owns = dp < Q_TILES
    t = jnp.minimum(dp, Q_TILES - 1)
    q_rows = pl.ds(pl.multiple_of((t // 7) * 8, 8), 8)
    q_lanes = pl.ds(pl.multiple_of((t % 7) * LANES, LANES), LANES)

    @pl.when(q_owns)
    def _():
        q_recv[dp] = q_raw[q_rows, q_lanes]
        got = q_recv.at[pl.ds(0, DPS - 1)]
        pltpu.make_async_copy(got, got, qs_recv).wait()
        q_full[q_rows, q_lanes] = jnp.sum(q_recv[...], axis=0)

        def send(d, carry):
            pltpu.make_async_remote_copy(
                src_ref=q_full.at[q_rows, q_lanes], dst_ref=q_full.at[q_rows, q_lanes],
                send_sem=qa_send, recv_sem=qa_recv, device_id=(dp_at(d), z), device_id_type=MESH).start()
            return carry
        lax.fori_loop(0, DPS - 1, send, 0)

    p_hat = mm(inv_left, six((psplit[:RANK, :], psplit[RANK:2 * RANK, :], psplit[2 * RANK:, :])))
    ph = jnp.transpose(p_hat)
    ph_hi, ph_lo = split2(ph)
    phat_ref[:, :RANK] = ph_hi
    phat_ref[:, RANK:2 * RANK] = ph_hi
    phat_ref[:, 2 * RANK:] = ph_lo
    q_hi, q_lo = split2(mm(inv_left, six(split3(q_raw[...]))))
    q_right = jnp.concatenate([q_hi, q_lo, q_hi], axis=0)
    for j in range(N_CHUNK):
        cols = pl.ds(j * CHUNK, CHUNK)
        c = c_hi[cols, :].astype(F32) + c_lo[cols, :].astype(F32)
        err_ref[cols, :] = (c - mm(phat_ref[cols, :], q_right)).astype(BF16)

    @pl.when(q_owns)
    def _():
        most = q_recv.at[pl.ds(0, Q_TILES - 1)]
        pltpu.make_async_copy(most, most, qa_recv).wait()

    @pl.when(jnp.logical_not(q_owns))
    def _():
        most = q_recv.at[pl.ds(0, Q_TILES)]
        pltpu.make_async_copy(most, most, qa_recv).wait()

    nextq_ref[...] = mm(inv_left, six(split3(q_full[...]))) * (1.0 / DPS)

    for j in range(N_CHUNK):
        core_copy(j).wait_send()

    @pl.when(owns)
    def _():
        sent = p_recv.at[pl.ds(0, P_TILES - 1)]
        pltpu.make_async_copy(sent, sent, rs_send).wait()
        sent = p_recv.at[pl.ds(0, CHIPS - 1)]
        pltpu.make_async_copy(sent, sent, ag_send).wait()

    @pl.when(jnp.logical_not(owns))
    def _():
        sent = p_recv.at[pl.ds(0, P_TILES)]
        pltpu.make_async_copy(sent, sent, rs_send).wait()

    @pl.when(q_owns)
    def _():
        sent = q_recv.at[pl.ds(0, Q_TILES - 1)]
        pltpu.make_async_copy(sent, sent, qs_send).wait()
        sent = q_recv.at[pl.ds(0, DPS - 1)]
        pltpu.make_async_copy(sent, sent, qa_send).wait()

    @pl.when(jnp.logical_not(q_owns))
    def _():
        sent = q_recv.at[pl.ds(0, Q_TILES)]
        pltpu.make_async_copy(sent, sent, qs_send).wait()


def factors(a, g, e, q):
    vm = pl.BlockSpec(memory_space=pltpu.VMEM)
    hbm = pl.BlockSpec(memory_space=pltpu.HBM)
    dma = pltpu.SemaphoreType.DMA
    return pl.pallas_call(
        body,
        out_shape=(
            pltpu.VMEM((ROWS, COLS), BF16),
            pltpu.VMEM((ROWS, 3 * RANK), BF16),
            pltpu.VMEM((RANK, COLS), F32),
        ),
        in_specs=[hbm, hbm, hbm, hbm],
        out_specs=(vm, vm, vm),
        scratch_shapes=[
            pltpu.VMEM((N_CHUNK, TOK, CHUNK), BF16),
            pltpu.VMEM((TOK, COLS), BF16),
            pltpu.VMEM((ROWS, COLS), BF16),
            pltpu.VMEM((RANK, COLS), F32),
            pltpu.VMEM((ROWS, COLS), BF16),
            pltpu.VMEM((ROWS, COLS), BF16),
            pltpu.VMEM((3 * RANK, COLS), BF16),
            pltpu.VMEM((3 * RANK, TOK), BF16),
            pltpu.VMEM((RANK, ROWS), F32),
            pltpu.VMEM((HALF, ROWS), F32),
            pltpu.VMEM((HALF, ROWS), F32),
            pltpu.VMEM((RANK, ROWS), F32),
            pltpu.VMEM((CHIPS, 8, LANES), F32),
            pltpu.VMEM((3 * RANK, ROWS), BF16),
            pltpu.VMEM((RANK, COLS), F32),
            pltpu.VMEM((DPS, 8, LANES), F32),
            pltpu.VMEM((RANK, COLS), F32),
            dma((N_CHUNK,)), dma, dma((N_CHUNK,)), dma, dma((N_CHUNK,)), dma((N_CHUNK,)),
            dma, dma, dma, dma, dma, dma, dma, dma, dma, dma,
        ],
        compiler_params=pltpu.CompilerParams(
            collective_id=0, has_side_effects=True, vmem_limit_bytes=54 * 2**20),
        name="factors",
    )(a, g, e, q)


def out_body(err_vm, phat_ref, nextq_ref, upd_hbm, err_hbm, nq_ref, upd_buf, err_sem, upd_sem):
    err_copy = pltpu.make_async_copy(err_vm, err_hbm, err_sem)
    err_copy.start()
    nq_ref[...] = nextq_ref[...]
    hi, lo = split2(nextq_ref[...])
    right = jnp.concatenate([hi, lo, hi], axis=0)
    copies = []
    for j in range(N_CHUNK):
        rows = pl.ds(j * CHUNK, CHUNK)
        upd_buf[rows, :] = mm(phat_ref[rows, :], right).astype(BF16)
        copies.append(pltpu.make_async_copy(upd_buf.at[rows, :], upd_hbm.at[rows, :], upd_sem.at[j]))
        copies[j].start()
    err_copy.wait()
    for copy in copies:
        copy.wait()


def outputs(err, phat, nextq):
    vm = pl.BlockSpec(memory_space=pltpu.VMEM)
    hbm = pl.BlockSpec(memory_space=pltpu.HBM)
    return pl.pallas_call(
        out_body,
        out_shape=(
            jax.ShapeDtypeStruct((ROWS, COLS), BF16),
            jax.ShapeDtypeStruct((ROWS, COLS), BF16),
            jax.ShapeDtypeStruct((RANK, COLS), F32),
        ),
        in_specs=[vm, vm, vm],
        out_specs=(hbm, hbm, vm),
        scratch_shapes=[
            pltpu.VMEM((ROWS, COLS), BF16),
            pltpu.SemaphoreType.DMA,
            pltpu.SemaphoreType.DMA((N_CHUNK,)),
        ],
        compiler_params=pltpu.CompilerParams(vmem_limit_bytes=40 * 2**20),
        name="outputs",
    )(err, phat, nextq)


def shards(activations, out_grads, error_buffer, basis_q):
    err, phat, nextq = factors(activations, out_grads, error_buffer[0], basis_q.T)
    update, new_error, next_q = outputs(err, phat, nextq)
    return update, new_error[None], next_q.T


def solution(mesh):
    in_specs = (P("dp", None), P("dp", "tensor"), P("dp", None, "tensor"), P("tensor", None))
    out_specs = (P(None, "tensor"), P("dp", None, "tensor"), P("tensor", None))
    return jax.shard_map(shards, mesh=mesh, in_specs=in_specs, out_specs=out_specs, check_vma=False)
```

```python
import jax
import jax.numpy as jnp
from jax import lax
from jax.experimental import pallas as pl
from jax.experimental.pallas import tpu as pltpu
from jax.sharding import PartitionSpec as P

MESH = pl.DeviceIdType.MESH
F32 = jnp.float32
BF16 = jnp.bfloat16

ROWS = 3584
COLS = 896
TOK = 1024
RANK = 32
HALF = RANK // 2
CHUNK = 512
N_CHUNK = ROWS // CHUNK
CHIPS = 64
DPS = 32
LANES = 128
P_TILES = 56
Q_TILES = 28
SCALE = 1.0 / 32.0
G_PARTS = 4
BAR_AT = 6
EARLY = 4
CUT = 14

NN = (((1,), (0,)), ((), ()))
NT = (((1,), (1,)), ((), ()))
TN = (((0,), (0,)), ((), ()))


def mm(a, b, dims=NN):
    return lax.dot_general(a, b, dims, preferred_element_type=F32)


def split2(x):
    hi = x.astype(BF16)
    lo = (x - hi.astype(F32)).astype(BF16)
    return hi, lo


def split3(x):
    hi = x.astype(BF16)
    rest = x - hi.astype(F32)
    mid = rest.astype(BF16)
    lo = (rest - mid.astype(F32)).astype(BF16)
    return hi, mid, lo


def fold3(x):
    return x[:RANK] + x[RANK:2 * RANK] + x[2 * RANK:]


def eliminate(work, scale, first, last):
    row_id = lax.broadcasted_iota(jnp.int32, (RANK, LANES), 0)
    for j in range(first, last):
        row = work[j:j + 1, :]
        piv = jnp.broadcast_to(work[j:j + 1, j:j + 1], (1, LANES))
        col = jnp.broadcast_to(work[:, j:j + 1], (RANK, LANES))
        scale = jnp.where(row_id == j, piv, scale)
        work = work - jnp.where(row_id > j, col * (row / piv), 0.0)
    return work, scale


def far(i):
    return jnp.where(i < 2, 2 + i, 3 - i)


def body(a_hbm, g_hbm, e_hbm, q_hbm, err_ref, phat_ref, nextq_ref,
         a_buf, g_buf, e_buf, q_buf, c_parts, qs, gqs, p_loc, core_buf, p_sum, p_full, p_recv, psplit,
         q_raw, q_recv, q_full,
         a_sem, g_sem, e_sem, q_sem, cs_sem, cr_sem, rs_send, rs_recv, ag_send, ag_recv,
         x_send, x_recv, qs_send, qs_recv, qa_send, qa_recv):
    dp = lax.axis_index("dp")
    z = lax.axis_index("tensor")
    core = dp % 2
    plane = dp // 2
    y = plane // 4
    x = plane % 4
    chip = plane * 4 + z
    sib = (plane * 2 + 1 - core, z)

    zs = tuple((z + step) % 4 for step in (2, 1, 3, 0))

    def plane_at(o):
        return ((y + far(o // 4)) % 4) * 4 + (x + far(o % 4)) % 4

    q_copy = pltpu.make_async_copy(q_hbm, q_buf, q_sem)
    q_copy.start()
    g_copies = []
    for i in range(G_PARTS):
        toks = pl.ds(i * (TOK // G_PARTS), TOK // G_PARTS)
        g_copies.append(pltpu.make_async_copy(g_hbm.at[toks, :], g_buf.at[toks, :], g_sem.at[i]))
        g_copies[i].start()
    a_copies = []
    e_copies = []
    for j in range(N_CHUNK):
        cols = pl.ds(j * CHUNK, CHUNK)
        a_copies.append(pltpu.make_async_copy(a_hbm.at[:, cols], a_buf.at[j], a_sem.at[j]))
        e_copies.append(pltpu.make_async_copy(e_hbm.at[cols, :], e_buf.at[cols, :], e_sem.at[j]))
    a_copies[0].start()
    e_copies[0].start()

    bar = pltpu.get_barrier_semaphore()

    def greet(there):
        pl.semaphore_signal(bar, inc=1, device_id=there, device_id_type=MESH)

    def greet_planes(first, last):
        def one(o, carry):
            there = plane_at(o) * 2
            for pz in zs:
                greet((there + core, pz))
            greet((there + 1 - core, z))
            return carry
        lax.fori_loop(first, last, one, 0)

    greet_planes(0, 11)

    q_copy.wait()
    for i, part in enumerate(split3(q_buf[...])):
        qs[i * RANK:(i + 1) * RANK, :] = part
    for i in range(G_PARTS):
        g_copies[i].wait()
    for j in range(1, N_CHUNK):
        a_copies[j].start()
        e_copies[j].start()
    greet_planes(11, 15)
    for pz in zs[:3]:
        greet((dp, pz))
    greet(sib)
    gq = fold3(mm(qs[...], g_buf[...], NT)) * SCALE
    for i, part in enumerate(split3(gq)):
        gqs[i * RANK:(i + 1) * RANK, :] = part

    mine = pl.multiple_of(core * HALF, HALF)
    other = pl.multiple_of(HALF - core * HALF, HALF)

    def core_copy(j):
        cols = pl.ds(j * CHUNK, CHUNK)
        return pltpu.make_async_remote_copy(
            src_ref=p_loc.at[pl.ds(other, HALF), cols], dst_ref=core_buf.at[:, cols],
            send_sem=cs_sem.at[j], recv_sem=cr_sem.at[j], device_id=sib, device_id_type=MESH)

    for j in range(N_CHUNK):
        cols = pl.ds(j * CHUNK, CHUNK)
        a_copies[j].wait()
        e_copies[j].wait()
        p_loc[:, cols] = fold3(mm(gqs[...], a_buf[j]) + mm(qs[...], e_buf[cols, :], NT))
        if j == BAR_AT:
            pl.semaphore_wait(bar, (CHIPS - 1) + (DPS // 2 - 1) + 1)
            for i in range(BAR_AT):
                core_copy(i).start()
        if j >= BAR_AT:
            core_copy(j).start()

    def tile(k):
        j = jnp.minimum(k % 8, N_CHUNK - 1)
        i = k // 8
        return pl.multiple_of((i // 4) * 8, 8), pl.ds(pl.multiple_of(j * CHUNK + (i % 4) * LANES, LANES), LANES)

    def scatter(odd, chunks):
        for j in chunks:
            cols = pl.ds(j * CHUNK, CHUNK)
            core_copy(j).wait_recv()
            p_sum[:, cols] = p_loc[pl.ds(mine, HALF), cols] + core_buf[:, cols]

        def send(o, carry):
            place = ((y + far(o // 2)) % 4) * 4 + ((x // 2 + 1 + o) % 2) * 2 + odd
            for pz in zs:
                k = place * 4 + pz
                first, lanes = tile(k)

                @pl.when(jnp.logical_and(k != chip, k % 8 < N_CHUNK))
                def _():
                    pltpu.make_async_remote_copy(
                        src_ref=p_sum.at[pl.ds(first, 8), lanes], dst_ref=p_recv.at[chip],
                        send_sem=rs_send, recv_sem=rs_recv,
                        device_id=(place * 2 + core, pz), device_id_type=MESH).start()
            return carry
        lax.fori_loop(0, 8, send, 0)

    scatter(0, range(4))
    scatter(1, range(4, N_CHUNK))

    def correct(j):
        cols = pl.ds(j * CHUNK, CHUNK)
        c = mm(a_buf[j], g_buf[...], TN) * SCALE + e_buf[cols, :].astype(F32)
        hi, lo = split2(c)
        c_parts[cols, :COLS] = hi
        c_parts[cols, COLS:COLS + LANES] = lo[:, COLS - LANES:]
        c_parts[cols, COLS + LANES:] = lo[:, :COLS - LANES]

    for j in range(EARLY):
        correct(j)

    t_j = chip % 8
    owns = t_j < N_CHUNK
    t_c = jnp.minimum(t_j, N_CHUNK - 1)
    t_first, t_lanes = tile(chip)
    t_rows = pl.ds(pl.multiple_of(core * HALF + t_first, 8), 8)

    @pl.when(owns)
    def _():
        p_recv[chip] = p_sum[pl.ds(t_first, 8), t_lanes]
        got = p_recv.at[pl.ds(0, CHIPS - 1)]
        pltpu.make_async_copy(got, got, rs_recv).wait()
        p_full[t_rows, t_lanes] = jnp.sum(p_recv[...], axis=0)

        def send(there):
            pltpu.make_async_remote_copy(
                src_ref=p_full.at[t_rows, t_lanes], dst_ref=p_full.at[t_rows, t_lanes],
                send_sem=ag_send, recv_sem=ag_recv.at[t_c],
                device_id=there, device_id_type=MESH).start()

        def send_plane(o, carry):
            there = plane_at(o) * 2 + core
            for pz in zs:
                send((there, pz))
            return carry
        lax.fori_loop(0, 15, send_plane, 0)
        for pz in zs[:3]:
            send((dp, pz))

    for j in range(EARLY, N_CHUNK):
        correct(j)

    def swap(j):
        part = p_full.at[pl.ds(mine, HALF), pl.ds(j * CHUNK, CHUNK)]
        return pltpu.make_async_remote_copy(
            src_ref=part, dst_ref=part, send_sem=x_send.at[j], recv_sem=x_recv.at[j],
            device_id=sib, device_id_type=MESH)

    for j in range(N_CHUNK):
        @pl.when(t_j == j)
        def _():
            most = p_recv.at[pl.ds(0, 7)]
            pltpu.make_async_copy(most, most, ag_recv.at[j]).wait()

        @pl.when(t_j != j)
        def _():
            most = p_recv.at[pl.ds(0, 8)]
            pltpu.make_async_copy(most, most, ag_recv.at[j]).wait()
        swap(j).start()
    for j in range(N_CHUNK):
        swap(j).wait_recv()

    for i, part in enumerate(split3(p_full[...])):
        psplit[i * RANK:(i + 1) * RANK, :] = part
    for first, tiles in ((0, 2), (2, 2), (4, 2), (6, 1)):
        cols = pl.ds(first * LANES, tiles * LANES)
        if tiles == 2:
            low = pl.ds(COLS + (first + 1) * LANES, tiles * LANES)
            q_raw[:, cols] = fold3(mm(psplit[...], c_parts[:, cols]) + mm(psplit[...], c_parts[:, low]))
        else:
            both = fold3(mm(psplit[...], c_parts[:, COLS - LANES:COLS + LANES]))
            q_raw[:, cols] = both[:, :LANES] + both[:, LANES:]

        def q_send(n, carry):
            t = first * 4 + (n + plane) % (tiles * 4)
            rows = pl.ds(pl.multiple_of((t % 4) * 8, 8), 8)
            lanes = pl.ds(pl.multiple_of((t // 4) * LANES, LANES), LANES)

            @pl.when(t != dp)
            def _():
                pltpu.make_async_remote_copy(
                    src_ref=q_raw.at[rows, lanes], dst_ref=q_recv.at[dp],
                    send_sem=qs_send, recv_sem=qs_recv, device_id=(t, z), device_id_type=MESH).start()

            @pl.when(t == dp)
            def _():
                q_recv[dp] = q_raw[rows, lanes]
            return carry
        lax.fori_loop(0, tiles * 4, q_send, 0)

    gram9 = mm(psplit[...], psplit[...], NT)
    gram = jnp.zeros((RANK, RANK), F32)
    for r in range(3):
        for c in range(3):
            gram = gram + gram9[r * RANK:(r + 1) * RANK, c * RANK:(c + 1) * RANK]
    row_id = lax.broadcasted_iota(jnp.int32, (RANK, LANES), 0)
    lane_id = lax.broadcasted_iota(jnp.int32, (RANK, LANES), 1)
    work = jnp.concatenate([gram, jnp.zeros((RANK, LANES - RANK), F32)], axis=1)
    work = work + (lane_id == row_id + RANK).astype(F32)
    work, scale = eliminate(work, jnp.zeros((RANK, LANES), F32), 0, CUT)
    q_owns = dp < Q_TILES
    t = jnp.minimum(dp, Q_TILES - 1)
    q_rows = pl.ds(pl.multiple_of((t % 4) * 8, 8), 8)
    q_lanes = pl.ds(pl.multiple_of((t // 4) * LANES, LANES), LANES)

    @pl.when(q_owns)
    def _():
        got = q_recv.at[pl.ds(0, DPS - 1)]
        pltpu.make_async_copy(got, got, qs_recv).wait()
        q_full[q_rows, q_lanes] = jnp.sum(q_recv[...], axis=0)

        def send(there):
            pltpu.make_async_remote_copy(
                src_ref=q_full.at[q_rows, q_lanes], dst_ref=q_full.at[q_rows, q_lanes],
                send_sem=qa_send, recv_sem=qa_recv, device_id=(there, z), device_id_type=MESH).start()

        def send_plane(o, carry):
            there = plane_at(o) * 2
            send(there + core)
            send(there + 1 - core)
            return carry
        lax.fori_loop(0, 15, send_plane, 0)
        send(plane * 2 + 1 - core)

    work, scale = eliminate(work, scale, CUT, RANK)
    inv = (work * lax.rsqrt(scale))[:, RANK:2 * RANK]
    inv_parts = split3(inv)
    inv_left = jnp.concatenate([inv_parts[0], inv_parts[0], inv_parts[1], inv_parts[0], inv_parts[1], inv_parts[2]], axis=1)

    def six(parts):
        return jnp.concatenate([parts[0], parts[1], parts[0], parts[2], parts[1], parts[0]], axis=0)

    p_hat = mm(inv_left, six((psplit[:RANK, :], psplit[RANK:2 * RANK, :], psplit[2 * RANK:, :])))
    ph = jnp.transpose(p_hat)
    ph_hi, ph_lo = split2(ph)
    phat_ref[:, :RANK] = ph_hi
    phat_ref[:, RANK:2 * RANK] = ph_hi
    phat_ref[:, 2 * RANK:] = ph_lo
    q_hi, q_lo = split2(mm(inv_left, six(split3(q_raw[...]))))
    q_right = jnp.concatenate([q_hi, q_lo, q_hi], axis=0)
    for j in range(N_CHUNK):
        cols = pl.ds(j * CHUNK, CHUNK)
        lo = jnp.concatenate([c_parts[cols, COLS + LANES:], c_parts[cols, COLS:COLS + LANES]], axis=1)
        c = c_parts[cols, :COLS].astype(F32) + lo.astype(F32)
        err_ref[cols, :] = (c - mm(phat_ref[cols, :], q_right)).astype(BF16)

    @pl.when(q_owns)
    def _():
        most = q_recv.at[pl.ds(0, Q_TILES - 1)]
        pltpu.make_async_copy(most, most, qa_recv).wait()

    @pl.when(jnp.logical_not(q_owns))
    def _():
        most = q_recv.at[pl.ds(0, Q_TILES)]
        pltpu.make_async_copy(most, most, qa_recv).wait()

    nextq_ref[...] = mm(inv_left, six(split3(q_full[...]))) * (1.0 / DPS)

    for j in range(N_CHUNK):
        core_copy(j).wait_send()
        swap(j).wait_send()

    @pl.when(owns)
    def _():
        sent = p_recv.at[pl.ds(0, P_TILES - 1)]
        pltpu.make_async_copy(sent, sent, rs_send).wait()
        sent = p_recv.at[pl.ds(0, CHIPS - 1)]
        pltpu.make_async_copy(sent, sent, ag_send).wait()

    @pl.when(jnp.logical_not(owns))
    def _():
        sent = p_recv.at[pl.ds(0, P_TILES)]
        pltpu.make_async_copy(sent, sent, rs_send).wait()

    @pl.when(q_owns)
    def _():
        sent = q_recv.at[pl.ds(0, Q_TILES - 1)]
        pltpu.make_async_copy(sent, sent, qs_send).wait()
        sent = q_recv.at[pl.ds(0, DPS - 1)]
        pltpu.make_async_copy(sent, sent, qa_send).wait()

    @pl.when(jnp.logical_not(q_owns))
    def _():
        sent = q_recv.at[pl.ds(0, Q_TILES)]
        pltpu.make_async_copy(sent, sent, qs_send).wait()


def factors(a, g, e, q):
    vm = pl.BlockSpec(memory_space=pltpu.VMEM)
    hbm = pl.BlockSpec(memory_space=pltpu.HBM)
    dma = pltpu.SemaphoreType.DMA
    return pl.pallas_call(
        body,
        out_shape=(
            pltpu.VMEM((ROWS, COLS), BF16),
            pltpu.VMEM((ROWS, 3 * RANK), BF16),
            pltpu.VMEM((RANK, COLS), F32),
        ),
        in_specs=[hbm, hbm, hbm, hbm],
        out_specs=(vm, vm, vm),
        scratch_shapes=[
            pltpu.VMEM((N_CHUNK, TOK, CHUNK), BF16),
            pltpu.VMEM((TOK, COLS), BF16),
            pltpu.VMEM((ROWS, COLS), BF16),
            pltpu.VMEM((RANK, COLS), F32),
            pltpu.VMEM((ROWS, 2 * COLS), BF16),
            pltpu.VMEM((3 * RANK, COLS), BF16),
            pltpu.VMEM((3 * RANK, TOK), BF16),
            pltpu.VMEM((RANK, ROWS), F32),
            pltpu.VMEM((HALF, ROWS), F32),
            pltpu.VMEM((HALF, ROWS), F32),
            pltpu.VMEM((RANK, ROWS), F32),
            pltpu.VMEM((CHIPS, 8, LANES), F32),
            pltpu.VMEM((3 * RANK, ROWS), BF16),
            pltpu.VMEM((RANK, COLS), F32),
            pltpu.VMEM((DPS, 8, LANES), F32),
            pltpu.VMEM((RANK, COLS), F32),
            dma((N_CHUNK,)), dma((G_PARTS,)), dma((N_CHUNK,)), dma, dma((N_CHUNK,)), dma((N_CHUNK,)),
            dma, dma, dma, dma((N_CHUNK,)), dma((N_CHUNK,)), dma((N_CHUNK,)), dma, dma, dma, dma,
        ],
        compiler_params=pltpu.CompilerParams(
            collective_id=0, has_side_effects=True, vmem_limit_bytes=54 * 2**20),
        name="factors",
    )(a, g, e, q)


def out_body(err_vm, phat_ref, nextq_ref, upd_hbm, err_hbm, nq_ref, upd_buf, err_sem, upd_sem):
    err_copy = pltpu.make_async_copy(err_vm, err_hbm, err_sem)
    err_copy.start()
    nq_ref[...] = nextq_ref[...]
    hi, lo = split2(nextq_ref[...])
    right = jnp.concatenate([hi, lo, hi], axis=0)
    copies = []
    for j in range(N_CHUNK):
        rows = pl.ds(j * CHUNK, CHUNK)
        upd_buf[rows, :] = mm(phat_ref[rows, :], right).astype(BF16)
        copies.append(pltpu.make_async_copy(upd_buf.at[rows, :], upd_hbm.at[rows, :], upd_sem.at[j]))
        copies[j].start()
    err_copy.wait()
    for copy in copies:
        copy.wait()


def outputs(err, phat, nextq):
    vm = pl.BlockSpec(memory_space=pltpu.VMEM)
    hbm = pl.BlockSpec(memory_space=pltpu.HBM)
    return pl.pallas_call(
        out_body,
        out_shape=(
            jax.ShapeDtypeStruct((ROWS, COLS), BF16),
            jax.ShapeDtypeStruct((ROWS, COLS), BF16),
            jax.ShapeDtypeStruct((RANK, COLS), F32),
        ),
        in_specs=[vm, vm, vm],
        out_specs=(hbm, hbm, vm),
        scratch_shapes=[
            pltpu.VMEM((ROWS, COLS), BF16),
            pltpu.SemaphoreType.DMA,
            pltpu.SemaphoreType.DMA((N_CHUNK,)),
        ],
        compiler_params=pltpu.CompilerParams(vmem_limit_bytes=40 * 2**20),
        name="outputs",
    )(err, phat, nextq)


def shards(activations, out_grads, error_buffer, basis_q):
    err, phat, nextq = factors(activations, out_grads, error_buffer[0], basis_q.T)
    update, new_error, next_q = outputs(err, phat, nextq)
    return update, new_error[None], next_q.T


def solution(mesh):
    in_specs = (P("dp", None), P("dp", "tensor"), P("dp", None, "tensor"), P("tensor", None))
    out_specs = (P(None, "tensor"), P("dp", None, "tensor"), P("tensor", None))
    return jax.shard_map(shards, mesh=mesh, in_specs=in_specs, out_specs=out_specs, check_vma=False)
```

```python
import jax
import jax.numpy as jnp
from jax import lax
from jax.experimental import pallas as pl
from jax.experimental.pallas import tpu as pltpu
from jax.sharding import PartitionSpec as P

MESH = pl.DeviceIdType.MESH
F32 = jnp.float32
BF16 = jnp.bfloat16

ROWS = 3584
COLS = 896
TOK = 1024
RANK = 32
HALF = RANK // 2
CHUNK = 512
N_CHUNK = ROWS // CHUNK
CHIPS = 64
DPS = 32
LANES = 128
P_TILES = 56
Q_TILES = 28
SCALE = 1.0 / 32.0
G_PARTS = 4
BAR_AT = 4
EARLY = 4
CUT = 14
ERR_CUTS = 14
UPD_CUTS = 28

NN = (((1,), (0,)), ((), ()))
NT = (((1,), (1,)), ((), ()))
TN = (((0,), (0,)), ((), ()))


def mm(a, b, dims=NN):
    return lax.dot_general(a, b, dims, preferred_element_type=F32)


def split2(x):
    hi = x.astype(BF16)
    lo = (x - hi.astype(F32)).astype(BF16)
    return hi, lo


def split3(x):
    hi = x.astype(BF16)
    rest = x - hi.astype(F32)
    mid = rest.astype(BF16)
    lo = (rest - mid.astype(F32)).astype(BF16)
    return hi, mid, lo


def fold3(x):
    return x[:RANK] + x[RANK:2 * RANK] + x[2 * RANK:]


def eliminate(work, scale, first, last):
    row_id = lax.broadcasted_iota(jnp.int32, (RANK, LANES), 0)
    for j in range(first, last):
        row = work[j:j + 1, :]
        piv = jnp.broadcast_to(work[j:j + 1, j:j + 1], (1, LANES))
        col = jnp.broadcast_to(work[:, j:j + 1], (RANK, LANES))
        scale = jnp.where(row_id == j, piv, scale)
        work = work - jnp.where(row_id > j, col * (row / piv), 0.0)
    return work, scale


def far(i):
    return jnp.where(i < 2, 2 + i, 3 - i)


def body(a_hbm, g_hbm, e_hbm, q_hbm, err_ref, phat_ref, nextq_ref,
         a_buf, g_buf, e_buf, q_buf, c_parts, qs, gqs, p_loc, core_buf, p_sum, p_full, p_recv, psplit,
         q_raw, q_recv, q_full,
         a_sem, g_sem, e_sem, q_sem, cs_sem, cr_sem, rs_send, rs_recv, ag_send, ag_recv,
         x_send, x_recv, qs_send, qs_recv, qa_send, qa_recv):
    dp = lax.axis_index("dp")
    z = lax.axis_index("tensor")
    core = dp % 2
    plane = dp // 2
    y = plane // 4
    x = plane % 4
    chip = plane * 4 + z
    sib = (plane * 2 + 1 - core, z)

    zs = tuple((z + step) % 4 for step in (2, 1, 3, 0))

    def plane_at(o):
        return ((y + far(o // 4)) % 4) * 4 + (x + far(o % 4)) % 4

    q_copy = pltpu.make_async_copy(q_hbm, q_buf, q_sem)
    q_copy.start()
    g_copies = []
    for i in range(G_PARTS):
        toks = pl.ds(i * (TOK // G_PARTS), TOK // G_PARTS)
        g_copies.append(pltpu.make_async_copy(g_hbm.at[toks, :], g_buf.at[toks, :], g_sem.at[i]))
        g_copies[i].start()
    a_copies = []
    e_copies = []
    for j in range(N_CHUNK):
        cols = pl.ds(j * CHUNK, CHUNK)
        a_copies.append(pltpu.make_async_copy(a_hbm.at[:, cols], a_buf.at[j], a_sem.at[j]))
        e_copies.append(pltpu.make_async_copy(e_hbm.at[cols, :], e_buf.at[cols, :], e_sem.at[j]))
    a_copies[0].start()
    e_copies[0].start()

    bar = pltpu.get_barrier_semaphore()

    def greet(there):
        pl.semaphore_signal(bar, inc=1, device_id=there, device_id_type=MESH)

    def greet_planes(first, last):
        def one(o, carry):
            there = plane_at(o) * 2
            for pz in zs:
                greet((there + core, pz))
            greet((there + 1 - core, z))
            return carry
        lax.fori_loop(first, last, one, 0)

    greet_planes(0, 11)

    q_copy.wait()
    for i, part in enumerate(split3(q_buf[...])):
        qs[i * RANK:(i + 1) * RANK, :] = part
    for i in range(G_PARTS):
        g_copies[i].wait()
    for j in range(1, N_CHUNK):
        a_copies[j].start()
        e_copies[j].start()
    greet_planes(11, 15)
    for pz in zs[:3]:
        greet((dp, pz))
    greet(sib)
    gq = fold3(mm(qs[...], g_buf[...], NT)) * SCALE
    for i, part in enumerate(split3(gq)):
        gqs[i * RANK:(i + 1) * RANK, :] = part

    mine = pl.multiple_of(core * HALF, HALF)
    other = pl.multiple_of(HALF - core * HALF, HALF)

    def core_copy(j):
        cols = pl.ds(j * CHUNK, CHUNK)
        return pltpu.make_async_remote_copy(
            src_ref=p_loc.at[pl.ds(other, HALF), cols], dst_ref=core_buf.at[:, cols],
            send_sem=cs_sem.at[j], recv_sem=cr_sem.at[j], device_id=sib, device_id_type=MESH)

    for j in range(N_CHUNK):
        cols = pl.ds(j * CHUNK, CHUNK)
        a_copies[j].wait()
        e_copies[j].wait()
        p_loc[:, cols] = fold3(mm(gqs[...], a_buf[j]) + mm(qs[...], e_buf[cols, :], NT))
        if j == BAR_AT:
            pl.semaphore_wait(bar, (CHIPS - 1) + (DPS // 2 - 1) + 1)
            for i in range(BAR_AT):
                core_copy(i).start()
        if j >= BAR_AT:
            core_copy(j).start()

    def tile(k):
        j = jnp.minimum(k % 8, N_CHUNK - 1)
        i = k // 8
        return pl.multiple_of((i // 4) * 8, 8), pl.ds(pl.multiple_of(j * CHUNK + (i % 4) * LANES, LANES), LANES)

    def scatter(odd, chunks):
        for j in chunks:
            cols = pl.ds(j * CHUNK, CHUNK)
            core_copy(j).wait_recv()
            p_sum[:, cols] = p_loc[pl.ds(mine, HALF), cols] + core_buf[:, cols]

        def send(o, carry):
            place = ((y + far(o // 2)) % 4) * 4 + ((x // 2 + 1 + o) % 2) * 2 + odd
            for pz in zs:
                k = place * 4 + pz
                first, lanes = tile(k)

                @pl.when(jnp.logical_and(k != chip, k % 8 < N_CHUNK))
                def _():
                    pltpu.make_async_remote_copy(
                        src_ref=p_sum.at[pl.ds(first, 8), lanes], dst_ref=p_recv.at[chip],
                        send_sem=rs_send, recv_sem=rs_recv,
                        device_id=(place * 2 + core, pz), device_id_type=MESH).start()
            return carry
        lax.fori_loop(0, 8, send, 0)

    scatter(0, range(4))
    scatter(1, range(4, N_CHUNK))

    def correct(j):
        cols = pl.ds(j * CHUNK, CHUNK)
        c = mm(a_buf[j], g_buf[...], TN) * SCALE + e_buf[cols, :].astype(F32)
        hi, lo = split2(c)
        c_parts[cols, :COLS] = hi
        c_parts[cols, COLS:COLS + LANES] = lo[:, COLS - LANES:]
        c_parts[cols, COLS + LANES:] = lo[:, :COLS - LANES]

    for j in range(EARLY):
        correct(j)

    t_j = chip % 8
    owns = t_j < N_CHUNK
    t_c = jnp.minimum(t_j, N_CHUNK - 1)
    t_first, t_lanes = tile(chip)
    t_rows = pl.ds(pl.multiple_of(core * HALF + t_first, 8), 8)

    @pl.when(owns)
    def _():
        p_recv[chip] = p_sum[pl.ds(t_first, 8), t_lanes]
        got = p_recv.at[pl.ds(0, CHIPS - 1)]
        pltpu.make_async_copy(got, got, rs_recv).wait()
        p_full[t_rows, t_lanes] = jnp.sum(p_recv[...], axis=0)

        def send(there):
            pltpu.make_async_remote_copy(
                src_ref=p_full.at[t_rows, t_lanes], dst_ref=p_full.at[t_rows, t_lanes],
                send_sem=ag_send, recv_sem=ag_recv.at[t_c],
                device_id=there, device_id_type=MESH).start()

        def send_plane(o, carry):
            there = plane_at(o) * 2 + core
            for pz in zs:
                send((there, pz))
            return carry
        lax.fori_loop(0, 15, send_plane, 0)
        for pz in zs[:3]:
            send((dp, pz))

    for j in range(EARLY, N_CHUNK):
        correct(j)

    def swap(j):
        part = p_full.at[pl.ds(mine, HALF), pl.ds(j * CHUNK, CHUNK)]
        return pltpu.make_async_remote_copy(
            src_ref=part, dst_ref=part, send_sem=x_send.at[j], recv_sem=x_recv.at[j],
            device_id=sib, device_id_type=MESH)

    for j in range(N_CHUNK):
        @pl.when(t_j == j)
        def _():
            most = p_recv.at[pl.ds(0, 7)]
            pltpu.make_async_copy(most, most, ag_recv.at[j]).wait()

        @pl.when(t_j != j)
        def _():
            most = p_recv.at[pl.ds(0, 8)]
            pltpu.make_async_copy(most, most, ag_recv.at[j]).wait()
        swap(j).start()
    def take(first, last):
        for j in range(first, last):
            swap(j).wait_recv()
        cols = pl.ds(first * CHUNK, (last - first) * CHUNK)
        for i, part in enumerate(split3(p_full[:, cols])):
            psplit[i * RANK:(i + 1) * RANK, cols] = part

    def product(rows, first, tiles):
        if tiles == 2:
            high = pl.ds(first * LANES, tiles * LANES)
            low = pl.ds(COLS + (first + 1) * LANES, tiles * LANES)
            return fold3(mm(psplit[:, rows], c_parts[rows, high]) + mm(psplit[:, rows], c_parts[rows, low]))
        both = fold3(mm(psplit[:, rows], c_parts[rows, COLS - LANES:COLS + LANES]))
        return both[:, :LANES] + both[:, LANES:]

    strips = ((0, 2), (2, 2), (4, 2), (6, 1))
    take(0, 4)
    for first, tiles in strips:
        q_raw[:, pl.ds(first * LANES, tiles * LANES)] = product(pl.ds(0, 4 * CHUNK), first, tiles)
    take(4, N_CHUNK)
    for first, tiles in strips:
        q_raw[:, pl.ds(first * LANES, tiles * LANES)] += product(pl.ds(4 * CHUNK, 3 * CHUNK), first, tiles)

        def q_send(n, carry):
            t = first * 4 + (n + plane) % (tiles * 4)
            rows = pl.ds(pl.multiple_of((t % 4) * 8, 8), 8)
            lanes = pl.ds(pl.multiple_of((t // 4) * LANES, LANES), LANES)

            @pl.when(t != dp)
            def _():
                pltpu.make_async_remote_copy(
                    src_ref=q_raw.at[rows, lanes], dst_ref=q_recv.at[dp],
                    send_sem=qs_send, recv_sem=qs_recv, device_id=(t, z), device_id_type=MESH).start()

            @pl.when(t == dp)
            def _():
                q_recv[dp] = q_raw[rows, lanes]
            return carry
        lax.fori_loop(0, tiles * 4, q_send, 0)

    gram9 = mm(psplit[...], psplit[...], NT)
    gram = jnp.zeros((RANK, RANK), F32)
    for r in range(3):
        for c in range(3):
            gram = gram + gram9[r * RANK:(r + 1) * RANK, c * RANK:(c + 1) * RANK]
    row_id = lax.broadcasted_iota(jnp.int32, (RANK, LANES), 0)
    lane_id = lax.broadcasted_iota(jnp.int32, (RANK, LANES), 1)
    work = jnp.concatenate([gram, jnp.zeros((RANK, LANES - RANK), F32)], axis=1)
    work = work + (lane_id == row_id + RANK).astype(F32)
    work, scale = eliminate(work, jnp.zeros((RANK, LANES), F32), 0, CUT)
    q_owns = dp < Q_TILES
    t = jnp.minimum(dp, Q_TILES - 1)
    q_rows = pl.ds(pl.multiple_of((t % 4) * 8, 8), 8)
    q_lanes = pl.ds(pl.multiple_of((t // 4) * LANES, LANES), LANES)

    @pl.when(q_owns)
    def _():
        got = q_recv.at[pl.ds(0, DPS - 1)]
        pltpu.make_async_copy(got, got, qs_recv).wait()
        q_full[q_rows, q_lanes] = jnp.sum(q_recv[...], axis=0)

        def send(there):
            pltpu.make_async_remote_copy(
                src_ref=q_full.at[q_rows, q_lanes], dst_ref=q_full.at[q_rows, q_lanes],
                send_sem=qa_send, recv_sem=qa_recv, device_id=(there, z), device_id_type=MESH).start()

        def send_plane(o, carry):
            there = plane_at(o) * 2
            send(there + core)
            send(there + 1 - core)
            return carry
        lax.fori_loop(0, 15, send_plane, 0)
        send(plane * 2 + 1 - core)

    work, scale = eliminate(work, scale, CUT, RANK)
    inv = (work * lax.rsqrt(scale))[:, RANK:2 * RANK]
    inv_parts = split3(inv)
    inv_left = jnp.concatenate([inv_parts[0], inv_parts[0], inv_parts[1], inv_parts[0], inv_parts[1], inv_parts[2]], axis=1)

    def six(parts):
        return jnp.concatenate([parts[0], parts[1], parts[0], parts[2], parts[1], parts[0]], axis=0)

    p_hat = mm(inv_left, six((psplit[:RANK, :], psplit[RANK:2 * RANK, :], psplit[2 * RANK:, :])))
    ph = jnp.transpose(p_hat)
    ph_hi, ph_lo = split2(ph)
    phat_ref[:, :RANK] = ph_hi
    phat_ref[:, RANK:2 * RANK] = ph_hi
    phat_ref[:, 2 * RANK:] = ph_lo
    q_hi, q_lo = split2(mm(inv_left, six(split3(q_raw[...]))))
    q_right = jnp.concatenate([q_hi, q_lo, q_hi], axis=0)
    for j in range(N_CHUNK):
        cols = pl.ds(j * CHUNK, CHUNK)
        lo = jnp.concatenate([c_parts[cols, COLS + LANES:], c_parts[cols, COLS:COLS + LANES]], axis=1)
        c = c_parts[cols, :COLS].astype(F32) + lo.astype(F32)
        err_ref[cols, :] = (c - mm(phat_ref[cols, :], q_right)).astype(BF16)

    @pl.when(q_owns)
    def _():
        most = q_recv.at[pl.ds(0, Q_TILES - 1)]
        pltpu.make_async_copy(most, most, qa_recv).wait()

    @pl.when(jnp.logical_not(q_owns))
    def _():
        most = q_recv.at[pl.ds(0, Q_TILES)]
        pltpu.make_async_copy(most, most, qa_recv).wait()

    nextq_ref[...] = mm(inv_left, six(split3(q_full[...]))) * (1.0 / DPS)

    for j in range(N_CHUNK):
        core_copy(j).wait_send()
        swap(j).wait_send()

    @pl.when(owns)
    def _():
        sent = p_recv.at[pl.ds(0, P_TILES - 1)]
        pltpu.make_async_copy(sent, sent, rs_send).wait()
        sent = p_recv.at[pl.ds(0, CHIPS - 1)]
        pltpu.make_async_copy(sent, sent, ag_send).wait()

    @pl.when(jnp.logical_not(owns))
    def _():
        sent = p_recv.at[pl.ds(0, P_TILES)]
        pltpu.make_async_copy(sent, sent, rs_send).wait()

    @pl.when(q_owns)
    def _():
        sent = q_recv.at[pl.ds(0, Q_TILES - 1)]
        pltpu.make_async_copy(sent, sent, qs_send).wait()
        sent = q_recv.at[pl.ds(0, DPS - 1)]
        pltpu.make_async_copy(sent, sent, qa_send).wait()

    @pl.when(jnp.logical_not(q_owns))
    def _():
        sent = q_recv.at[pl.ds(0, Q_TILES)]
        pltpu.make_async_copy(sent, sent, qs_send).wait()


def factors(a, g, e, q):
    vm = pl.BlockSpec(memory_space=pltpu.VMEM)
    hbm = pl.BlockSpec(memory_space=pltpu.HBM)
    dma = pltpu.SemaphoreType.DMA
    return pl.pallas_call(
        body,
        out_shape=(
            pltpu.VMEM((ROWS, COLS), BF16),
            pltpu.VMEM((ROWS, 3 * RANK), BF16),
            pltpu.VMEM((RANK, COLS), F32),
        ),
        in_specs=[hbm, hbm, hbm, hbm],
        out_specs=(vm, vm, vm),
        scratch_shapes=[
            pltpu.VMEM((N_CHUNK, TOK, CHUNK), BF16),
            pltpu.VMEM((TOK, COLS), BF16),
            pltpu.VMEM((ROWS, COLS), BF16),
            pltpu.VMEM((RANK, COLS), F32),
            pltpu.VMEM((ROWS, 2 * COLS), BF16),
            pltpu.VMEM((3 * RANK, COLS), BF16),
            pltpu.VMEM((3 * RANK, TOK), BF16),
            pltpu.VMEM((RANK, ROWS), F32),
            pltpu.VMEM((HALF, ROWS), F32),
            pltpu.VMEM((HALF, ROWS), F32),
            pltpu.VMEM((RANK, ROWS), F32),
            pltpu.VMEM((CHIPS, 8, LANES), F32),
            pltpu.VMEM((3 * RANK, ROWS), BF16),
            pltpu.VMEM((RANK, COLS), F32),
            pltpu.VMEM((DPS, 8, LANES), F32),
            pltpu.VMEM((RANK, COLS), F32),
            dma((N_CHUNK,)), dma((G_PARTS,)), dma((N_CHUNK,)), dma, dma((N_CHUNK,)), dma((N_CHUNK,)),
            dma, dma, dma, dma((N_CHUNK,)), dma((N_CHUNK,)), dma((N_CHUNK,)), dma, dma, dma, dma,
        ],
        compiler_params=pltpu.CompilerParams(
            collective_id=0, has_side_effects=True, vmem_limit_bytes=54 * 2**20),
        name="factors",
    )(a, g, e, q)


def out_body(err_vm, phat_ref, nextq_ref, upd_hbm, err_hbm, nq_ref, upd_buf, err_sem, upd_sem):
    copies = []

    def leave(src, dst, rows, sem):
        copies.append(pltpu.make_async_copy(src.at[rows, :], dst.at[rows, :], sem))
        copies[-1].start()

    for j in range(ERR_CUTS):
        leave(err_vm, err_hbm, pl.ds(j * (ROWS // ERR_CUTS), ROWS // ERR_CUTS), err_sem.at[j])
    nq_ref[...] = nextq_ref[...]
    hi, lo = split2(nextq_ref[...])
    right = jnp.concatenate([hi, lo, hi], axis=0)
    for j in range(UPD_CUTS):
        rows = pl.ds(j * (ROWS // UPD_CUTS), ROWS // UPD_CUTS)
        upd_buf[rows, :] = mm(phat_ref[rows, :], right).astype(BF16)
        leave(upd_buf, upd_hbm, rows, upd_sem.at[j])
    for copy in copies:
        copy.wait()


def outputs(err, phat, nextq):
    vm = pl.BlockSpec(memory_space=pltpu.VMEM)
    hbm = pl.BlockSpec(memory_space=pltpu.HBM)
    return pl.pallas_call(
        out_body,
        out_shape=(
            jax.ShapeDtypeStruct((ROWS, COLS), BF16),
            jax.ShapeDtypeStruct((ROWS, COLS), BF16),
            jax.ShapeDtypeStruct((RANK, COLS), F32),
        ),
        in_specs=[vm, vm, vm],
        out_specs=(hbm, hbm, vm),
        scratch_shapes=[
            pltpu.VMEM((ROWS, COLS), BF16),
            pltpu.SemaphoreType.DMA((ERR_CUTS,)),
            pltpu.SemaphoreType.DMA((UPD_CUTS,)),
        ],
        compiler_params=pltpu.CompilerParams(vmem_limit_bytes=40 * 2**20),
        name="outputs",
    )(err, phat, nextq)


def shards(activations, out_grads, error_buffer, basis_q):
    err, phat, nextq = factors(activations, out_grads, error_buffer[0], basis_q.T)
    update, new_error, next_q = outputs(err, phat, nextq)
    return update, new_error[None], next_q.T


def solution(mesh):
    in_specs = (P("dp", None), P("dp", "tensor"), P("dp", None, "tensor"), P("tensor", None))
    out_specs = (P(None, "tensor"), P("dp", None, "tensor"), P("tensor", None))
    return jax.shard_map(shards, mesh=mesh, in_specs=in_specs, out_specs=out_specs, check_vma=False)
```

```python
import jax
import jax.numpy as jnp
from jax import lax
from jax.experimental import pallas as pl
from jax.experimental.pallas import tpu as pltpu
from jax.sharding import PartitionSpec as P

MESH = pl.DeviceIdType.MESH
F32 = jnp.float32
BF16 = jnp.bfloat16

ROWS = 3584
COLS = 896
TOK = 1024
RANK = 32
HALF = RANK // 2
CHUNK = 512
N_CHUNK = ROWS // CHUNK
CHIPS = 64
DPS = 32
LANES = 128
P_TILES = 56
Q_TILES = 28
SCALE = 1.0 / 32.0
G_PARTS = 4
BAR_AT = 4
EARLY = 3
CUT = 14
ERR_CUTS = 14
UPD_CUTS = 28

NN = (((1,), (0,)), ((), ()))
NT = (((1,), (1,)), ((), ()))
TN = (((0,), (0,)), ((), ()))


def mm(a, b, dims=NN):
    return lax.dot_general(a, b, dims, preferred_element_type=F32)


def split2(x):
    hi = x.astype(BF16)
    lo = (x - hi.astype(F32)).astype(BF16)
    return hi, lo


def split3(x):
    hi = x.astype(BF16)
    rest = x - hi.astype(F32)
    mid = rest.astype(BF16)
    lo = (rest - mid.astype(F32)).astype(BF16)
    return hi, mid, lo


def fold3(x):
    return x[:RANK] + x[RANK:2 * RANK] + x[2 * RANK:]


def eliminate(work, scale, first, last):
    row_id = lax.broadcasted_iota(jnp.int32, (RANK, LANES), 0)
    for j in range(first, last):
        row = work[j:j + 1, :]
        piv = jnp.broadcast_to(work[j:j + 1, j:j + 1], (1, LANES))
        col = jnp.broadcast_to(work[:, j:j + 1], (RANK, LANES))
        scale = jnp.where(row_id == j, piv, scale)
        work = work - jnp.where(row_id > j, col * (row / piv), 0.0)
    return work, scale


def far(i):
    return jnp.where(i < 2, 2 + i, 3 - i)


def body(a_hbm, g_hbm, e_hbm, q_hbm, err_ref, phat_ref, nextq_ref,
         a_buf, g_buf, e_buf, q_buf, c_parts, qs, gqs, p_loc, core_buf, p_sum, p_full, p_recv, psplit,
         q_raw, q_recv, q_full,
         a_sem, g_sem, e_sem, q_sem, cs_sem, cr_sem, rs_send, rs_recv, ag_send, ag_recv,
         x_send, x_recv, qs_send, qs_recv, qa_send, qa_recv):
    dp = lax.axis_index("dp")
    z = lax.axis_index("tensor")
    core = dp % 2
    plane = dp // 2
    y = plane // 4
    x = plane % 4
    chip = plane * 4 + z
    sib = (plane * 2 + 1 - core, z)

    zs = tuple((z + step) % 4 for step in (2, 1, 3, 0))

    def plane_at(o):
        return ((y + far(o // 4)) % 4) * 4 + (x + far(o % 4)) % 4

    q_copy = pltpu.make_async_copy(q_hbm, q_buf, q_sem)
    q_copy.start()
    g_copies = []
    for i in range(G_PARTS):
        toks = pl.ds(i * (TOK // G_PARTS), TOK // G_PARTS)
        g_copies.append(pltpu.make_async_copy(g_hbm.at[toks, :], g_buf.at[toks, :], g_sem.at[i]))
        g_copies[i].start()
    a_copies = []
    e_copies = []
    for j in range(N_CHUNK):
        cols = pl.ds(j * CHUNK, CHUNK)
        a_copies.append(pltpu.make_async_copy(a_hbm.at[:, cols], a_buf.at[j], a_sem.at[j]))
        e_copies.append(pltpu.make_async_copy(e_hbm.at[cols, :], e_buf.at[cols, :], e_sem.at[j]))
    a_copies[0].start()
    e_copies[0].start()

    bar = pltpu.get_barrier_semaphore()

    def greet(there):
        pl.semaphore_signal(bar, inc=1, device_id=there, device_id_type=MESH)

    def greet_planes(first, last):
        def one(o, carry):
            there = plane_at(o) * 2
            for pz in zs:
                greet((there + core, pz))
            greet((there + 1 - core, z))
            return carry
        lax.fori_loop(first, last, one, 0)

    greet_planes(0, 11)

    q_copy.wait()
    for i, part in enumerate(split3(q_buf[...])):
        qs[i * RANK:(i + 1) * RANK, :] = part
    for i in range(G_PARTS):
        g_copies[i].wait()
    for j in range(1, N_CHUNK):
        a_copies[j].start()
        e_copies[j].start()
    greet_planes(11, 15)
    for pz in zs[:3]:
        greet((dp, pz))
    greet(sib)
    gq = fold3(mm(qs[...], g_buf[...], NT)) * SCALE
    for i, part in enumerate(split3(gq)):
        gqs[i * RANK:(i + 1) * RANK, :] = part

    mine = pl.multiple_of(core * HALF, HALF)
    other = pl.multiple_of(HALF - core * HALF, HALF)

    def core_copy(j):
        cols = pl.ds(j * CHUNK, CHUNK)
        return pltpu.make_async_remote_copy(
            src_ref=p_loc.at[pl.ds(other, HALF), cols], dst_ref=core_buf.at[:, cols],
            send_sem=cs_sem.at[j], recv_sem=cr_sem.at[j], device_id=sib, device_id_type=MESH)

    for j in range(N_CHUNK):
        cols = pl.ds(j * CHUNK, CHUNK)
        a_copies[j].wait()
        e_copies[j].wait()
        p_loc[:, cols] = fold3(mm(gqs[...], a_buf[j]) + mm(qs[...], e_buf[cols, :], NT))
        if j == BAR_AT:
            pl.semaphore_wait(bar, (CHIPS - 1) + (DPS // 2 - 1) + 1)
            for i in range(BAR_AT):
                core_copy(i).start()
        if j >= BAR_AT:
            core_copy(j).start()

    def tile(k):
        j = jnp.minimum(k % 8, N_CHUNK - 1)
        i = k // 8
        return pl.multiple_of((i // 4) * 8, 8), pl.ds(pl.multiple_of(j * CHUNK + (i % 4) * LANES, LANES), LANES)

    def scatter(odd, chunks):
        for j in chunks:
            cols = pl.ds(j * CHUNK, CHUNK)
            core_copy(j).wait_recv()
            p_sum[:, cols] = p_loc[pl.ds(mine, HALF), cols] + core_buf[:, cols]

        def send(o, carry):
            place = ((y + far(o // 2)) % 4) * 4 + ((x // 2 + 1 + o) % 2) * 2 + odd
            for pz in zs:
                k = place * 4 + pz
                first, lanes = tile(k)

                @pl.when(jnp.logical_and(k != chip, k % 8 < N_CHUNK))
                def _():
                    pltpu.make_async_remote_copy(
                        src_ref=p_sum.at[pl.ds(first, 8), lanes], dst_ref=p_recv.at[chip],
                        send_sem=rs_send, recv_sem=rs_recv,
                        device_id=(place * 2 + core, pz), device_id_type=MESH).start()
            return carry
        lax.fori_loop(0, 8, send, 0)

    scatter(0, range(4))
    scatter(1, range(4, N_CHUNK))

    def correct(j):
        cols = pl.ds(j * CHUNK, CHUNK)
        c = mm(a_buf[j], g_buf[...], TN) * SCALE + e_buf[cols, :].astype(F32)
        hi, lo = split2(c)
        c_parts[cols, :COLS] = hi
        c_parts[cols, COLS:COLS + LANES] = lo[:, COLS - LANES:]
        c_parts[cols, COLS + LANES:] = lo[:, :COLS - LANES]

    for j in range(EARLY):
        correct(j)

    t_j = chip % 8
    owns = t_j < N_CHUNK
    t_c = jnp.minimum(t_j, N_CHUNK - 1)
    t_first, t_lanes = tile(chip)
    t_rows = pl.ds(pl.multiple_of(core * HALF + t_first, 8), 8)

    @pl.when(owns)
    def _():
        p_recv[chip] = p_sum[pl.ds(t_first, 8), t_lanes]
        got = p_recv.at[pl.ds(0, CHIPS - 1)]
        pltpu.make_async_copy(got, got, rs_recv).wait()
        p_full[t_rows, t_lanes] = jnp.sum(p_recv[...], axis=0)

        def send(there):
            pltpu.make_async_remote_copy(
                src_ref=p_full.at[t_rows, t_lanes], dst_ref=p_full.at[t_rows, t_lanes],
                send_sem=ag_send, recv_sem=ag_recv.at[t_c],
                device_id=there, device_id_type=MESH).start()

        def send_plane(o, carry):
            there = plane_at(o) * 2 + core
            for pz in zs:
                send((there, pz))
            return carry
        lax.fori_loop(0, 15, send_plane, 0)
        for pz in zs[:3]:
            send((dp, pz))

    for j in range(EARLY, N_CHUNK):
        correct(j)

    def swap(j):
        part = p_full.at[pl.ds(mine, HALF), pl.ds(j * CHUNK, CHUNK)]
        return pltpu.make_async_remote_copy(
            src_ref=part, dst_ref=part, send_sem=x_send.at[j], recv_sem=x_recv.at[j],
            device_id=sib, device_id_type=MESH)

    for j in range(N_CHUNK):
        @pl.when(t_j == j)
        def _():
            most = p_recv.at[pl.ds(0, 7)]
            pltpu.make_async_copy(most, most, ag_recv.at[j]).wait()

        @pl.when(t_j != j)
        def _():
            most = p_recv.at[pl.ds(0, 8)]
            pltpu.make_async_copy(most, most, ag_recv.at[j]).wait()
        swap(j).start()
    def take(first, last):
        for j in range(first, last):
            swap(j).wait_recv()
        cols = pl.ds(first * CHUNK, (last - first) * CHUNK)
        for i, part in enumerate(split3(p_full[:, cols])):
            psplit[i * RANK:(i + 1) * RANK, cols] = part

    def product(rows, first, tiles):
        if tiles == 2:
            high = pl.ds(first * LANES, tiles * LANES)
            low = pl.ds(COLS + (first + 1) * LANES, tiles * LANES)
            return fold3(mm(psplit[:, rows], c_parts[rows, high]) + mm(psplit[:, rows], c_parts[rows, low]))
        both = fold3(mm(psplit[:, rows], c_parts[rows, COLS - LANES:COLS + LANES]))
        return both[:, :LANES] + both[:, LANES:]

    strips = ((0, 2), (2, 2), (4, 2), (6, 1))
    take(0, 4)
    for first, tiles in strips:
        q_raw[:, pl.ds(first * LANES, tiles * LANES)] = product(pl.ds(0, 4 * CHUNK), first, tiles)
    take(4, N_CHUNK)
    for first, tiles in strips:
        q_raw[:, pl.ds(first * LANES, tiles * LANES)] += product(pl.ds(4 * CHUNK, 3 * CHUNK), first, tiles)

        def q_send(n, carry):
            t = first * 4 + (n + plane) % (tiles * 4)
            rows = pl.ds(pl.multiple_of((t % 4) * 8, 8), 8)
            lanes = pl.ds(pl.multiple_of((t // 4) * LANES, LANES), LANES)

            @pl.when(t != dp)
            def _():
                pltpu.make_async_remote_copy(
                    src_ref=q_raw.at[rows, lanes], dst_ref=q_recv.at[dp],
                    send_sem=qs_send, recv_sem=qs_recv, device_id=(t, z), device_id_type=MESH).start()

            @pl.when(t == dp)
            def _():
                q_recv[dp] = q_raw[rows, lanes]
            return carry
        lax.fori_loop(0, tiles * 4, q_send, 0)

    gram9 = mm(psplit[...], psplit[...], NT)
    gram = jnp.zeros((RANK, RANK), F32)
    for r in range(3):
        for c in range(3):
            gram = gram + gram9[r * RANK:(r + 1) * RANK, c * RANK:(c + 1) * RANK]
    row_id = lax.broadcasted_iota(jnp.int32, (RANK, LANES), 0)
    lane_id = lax.broadcasted_iota(jnp.int32, (RANK, LANES), 1)
    work = jnp.concatenate([gram, jnp.zeros((RANK, LANES - RANK), F32)], axis=1)
    work = work + (lane_id == row_id + RANK).astype(F32)
    work, scale = eliminate(work, jnp.zeros((RANK, LANES), F32), 0, CUT)
    q_owns = dp < Q_TILES
    t = jnp.minimum(dp, Q_TILES - 1)
    q_rows = pl.ds(pl.multiple_of((t % 4) * 8, 8), 8)
    q_lanes = pl.ds(pl.multiple_of((t // 4) * LANES, LANES), LANES)

    @pl.when(q_owns)
    def _():
        got = q_recv.at[pl.ds(0, DPS - 1)]
        pltpu.make_async_copy(got, got, qs_recv).wait()
        q_full[q_rows, q_lanes] = jnp.sum(q_recv[...], axis=0)

        def send(there):
            pltpu.make_async_remote_copy(
                src_ref=q_full.at[q_rows, q_lanes], dst_ref=q_full.at[q_rows, q_lanes],
                send_sem=qa_send, recv_sem=qa_recv, device_id=(there, z), device_id_type=MESH).start()

        def send_plane(o, carry):
            there = plane_at(o) * 2
            send(there + core)
            send(there + 1 - core)
            return carry
        lax.fori_loop(0, 15, send_plane, 0)
        send(plane * 2 + 1 - core)

    work, scale = eliminate(work, scale, CUT, RANK)
    inv = (work * lax.rsqrt(scale))[:, RANK:2 * RANK]
    inv_parts = split3(inv)
    inv_left = jnp.concatenate([inv_parts[0], inv_parts[0], inv_parts[1], inv_parts[0], inv_parts[1], inv_parts[2]], axis=1)

    def six(parts):
        return jnp.concatenate([parts[0], parts[1], parts[0], parts[2], parts[1], parts[0]], axis=0)

    p_hat = mm(inv_left, six((psplit[:RANK, :], psplit[RANK:2 * RANK, :], psplit[2 * RANK:, :])))
    ph = jnp.transpose(p_hat)
    ph_hi, ph_lo = split2(ph)
    phat_ref[:, :RANK] = ph_hi
    phat_ref[:, RANK:2 * RANK] = ph_hi
    phat_ref[:, 2 * RANK:] = ph_lo
    q_hi, q_lo = split2(mm(inv_left, six(split3(q_raw[...]))))
    q_right = jnp.concatenate([q_hi, q_lo, q_hi], axis=0)
    for j in range(N_CHUNK):
        cols = pl.ds(j * CHUNK, CHUNK)
        lo = jnp.concatenate([c_parts[cols, COLS + LANES:], c_parts[cols, COLS:COLS + LANES]], axis=1)
        c = c_parts[cols, :COLS].astype(F32) + lo.astype(F32)
        err_ref[cols, :] = (c - mm(phat_ref[cols, :], q_right)).astype(BF16)

    @pl.when(q_owns)
    def _():
        most = q_recv.at[pl.ds(0, Q_TILES - 1)]
        pltpu.make_async_copy(most, most, qa_recv).wait()

    @pl.when(jnp.logical_not(q_owns))
    def _():
        most = q_recv.at[pl.ds(0, Q_TILES)]
        pltpu.make_async_copy(most, most, qa_recv).wait()

    nextq_ref[...] = mm(inv_left, six(split3(q_full[...]))) * (1.0 / DPS)

    for j in range(N_CHUNK):
        core_copy(j).wait_send()
        swap(j).wait_send()

    @pl.when(owns)
    def _():
        sent = p_recv.at[pl.ds(0, P_TILES - 1)]
        pltpu.make_async_copy(sent, sent, rs_send).wait()
        sent = p_recv.at[pl.ds(0, CHIPS - 1)]
        pltpu.make_async_copy(sent, sent, ag_send).wait()

    @pl.when(jnp.logical_not(owns))
    def _():
        sent = p_recv.at[pl.ds(0, P_TILES)]
        pltpu.make_async_copy(sent, sent, rs_send).wait()

    @pl.when(q_owns)
    def _():
        sent = q_recv.at[pl.ds(0, Q_TILES - 1)]
        pltpu.make_async_copy(sent, sent, qs_send).wait()
        sent = q_recv.at[pl.ds(0, DPS - 1)]
        pltpu.make_async_copy(sent, sent, qa_send).wait()

    @pl.when(jnp.logical_not(q_owns))
    def _():
        sent = q_recv.at[pl.ds(0, Q_TILES)]
        pltpu.make_async_copy(sent, sent, qs_send).wait()


def factors(a, g, e, q):
    vm = pl.BlockSpec(memory_space=pltpu.VMEM)
    hbm = pl.BlockSpec(memory_space=pltpu.HBM)
    dma = pltpu.SemaphoreType.DMA
    return pl.pallas_call(
        body,
        out_shape=(
            pltpu.VMEM((ROWS, COLS), BF16),
            pltpu.VMEM((ROWS, 3 * RANK), BF16),
            pltpu.VMEM((RANK, COLS), F32),
        ),
        in_specs=[hbm, hbm, hbm, hbm],
        out_specs=(vm, vm, vm),
        scratch_shapes=[
            pltpu.VMEM((N_CHUNK, TOK, CHUNK), BF16),
            pltpu.VMEM((TOK, COLS), BF16),
            pltpu.VMEM((ROWS, COLS), BF16),
            pltpu.VMEM((RANK, COLS), F32),
            pltpu.VMEM((ROWS, 2 * COLS), BF16),
            pltpu.VMEM((3 * RANK, COLS), BF16),
            pltpu.VMEM((3 * RANK, TOK), BF16),
            pltpu.VMEM((RANK, ROWS), F32),
            pltpu.VMEM((HALF, ROWS), F32),
            pltpu.VMEM((HALF, ROWS), F32),
            pltpu.VMEM((RANK, ROWS), F32),
            pltpu.VMEM((CHIPS, 8, LANES), F32),
            pltpu.VMEM((3 * RANK, ROWS), BF16),
            pltpu.VMEM((RANK, COLS), F32),
            pltpu.VMEM((DPS, 8, LANES), F32),
            pltpu.VMEM((RANK, COLS), F32),
            dma((N_CHUNK,)), dma((G_PARTS,)), dma((N_CHUNK,)), dma, dma((N_CHUNK,)), dma((N_CHUNK,)),
            dma, dma, dma, dma((N_CHUNK,)), dma((N_CHUNK,)), dma((N_CHUNK,)), dma, dma, dma, dma,
        ],
        compiler_params=pltpu.CompilerParams(
            collective_id=0, has_side_effects=True, vmem_limit_bytes=54 * 2**20),
        name="factors",
    )(a, g, e, q)


def out_body(err_vm, phat_ref, nextq_ref, upd_hbm, err_hbm, nq_hbm, upd_buf, err_sem, upd_sem, nq_sem):
    copies = []

    def leave(src, dst, rows, sem):
        copies.append(pltpu.make_async_copy(src.at[rows, :], dst.at[rows, :], sem))
        copies[-1].start()

    for j in range(ERR_CUTS):
        leave(err_vm, err_hbm, pl.ds(j * (ROWS // ERR_CUTS), ROWS // ERR_CUTS), err_sem.at[j])
    copies.append(pltpu.make_async_copy(nextq_ref, nq_hbm, nq_sem))
    copies[-1].start()
    hi, lo = split2(nextq_ref[...])
    right = jnp.concatenate([hi, lo, hi], axis=0)
    for j in range(UPD_CUTS):
        rows = pl.ds(j * (ROWS // UPD_CUTS), ROWS // UPD_CUTS)
        upd_buf[rows, :] = mm(phat_ref[rows, :], right).astype(BF16)
        leave(upd_buf, upd_hbm, rows, upd_sem.at[j])
    for copy in copies:
        copy.wait()


def outputs(err, phat, nextq):
    vm = pl.BlockSpec(memory_space=pltpu.VMEM)
    hbm = pl.BlockSpec(memory_space=pltpu.HBM)
    return pl.pallas_call(
        out_body,
        out_shape=(
            jax.ShapeDtypeStruct((ROWS, COLS), BF16),
            jax.ShapeDtypeStruct((ROWS, COLS), BF16),
            jax.ShapeDtypeStruct((RANK, COLS), F32),
        ),
        in_specs=[vm, vm, vm],
        out_specs=(hbm, hbm, hbm),
        scratch_shapes=[
            pltpu.VMEM((ROWS, COLS), BF16),
            pltpu.SemaphoreType.DMA((ERR_CUTS,)),
            pltpu.SemaphoreType.DMA((UPD_CUTS,)),
            pltpu.SemaphoreType.DMA,
        ],
        compiler_params=pltpu.CompilerParams(vmem_limit_bytes=40 * 2**20),
        name="outputs",
    )(err, phat, nextq)


def shards(activations, out_grads, error_buffer, basis_q):
    err, phat, nextq = factors(activations, out_grads, error_buffer[0], basis_q.T)
    update, new_error, next_q = outputs(err, phat, nextq)
    return update, new_error[None], next_q.T


def solution(mesh):
    in_specs = (P("dp", None), P("dp", "tensor"), P("dp", None, "tensor"), P("tensor", None))
    out_specs = (P(None, "tensor"), P("dp", None, "tensor"), P("tensor", None))
    return jax.shard_map(shards, mesh=mesh, in_specs=in_specs, out_specs=out_specs, check_vma=False)
```
